128 devices in a mesh: dp: 16 (over z, x), space: 8 (over y, core).
Axes of the slice: x: 4, y: 4, z: 4, core: 2. Of those that a mesh axis runs over, the one named last changes fastest.
Arguments:
- field: bfloat16 [32, 64, 64, 4096], P('dp', 'space'), may hold values from -6 to 6
- cotangent: bfloat16 [32, 64, 64, 4096], P('dp', 'space'), may hold values from -6 to 6
- spectral_weight: bfloat16 [256, 16, 64, 128], P('dp', 'space'), may hold values from -0.5 to 0.5
- point_weight: bfloat16 [64, 64], replicated, may hold values from -0.75 to 0.75
- bias: float32 [64], replicated, may hold values from -3 to 3
Outputs:
- field_grad: bfloat16 [32, 64, 64, 4096], P('dp', 'space')
- weight_grad: float32 [256, 16, 64, 128], P('dp', 'space')
The draws below stay inside these ranges and needn't reach their ends.
All inputs are finite; a program needn't handle non-finite values.
Results may differ from the reference program's by a relative error of at most 0.023.
Values may be sent and summed in bfloat16 or wider, within the bound.
A program may use at most 320 MiB of HBM per device.

```python
import math
import jax
import jax.numpy as jnp
from jax import lax

C = 64
K = 16
G = 64
SAMPLES = 32


def shard_levels(rng, dims, cuts, low, top_value):
    def one(axis_at, shards_of):
        heights = jax.random.uniform(jax.random.fold_in(jax.random.fold_in(rng, 6), axis_at), (shards_of,), jnp.float32, low / len(cuts), top_value / len(cuts))
        return jnp.repeat(jnp.exp(heights), dims[axis_at] // shards_of).reshape((-1,) + (1,) * (len(dims) - axis_at - 1))

    factor_of = one(*cuts[0])
    for cut in cuts[1:]:
        factor_of = factor_of * one(*cut)
    return factor_of


def gaussian(rng, shape, spread, bound, pieces=(), kind=jnp.bfloat16):
    values = jax.random.normal(rng, shape, jnp.float32) * spread
    if len(pieces) > 0:
        values = shard_levels(rng, shape, pieces, -0.22, 0.18) * values
    return jnp.clip(values, min=-bound, max=bound).astype(kind)


def setup_inputs(seed: int = 0) -> dict:
    keys = jax.random.split(jax.random.key(seed), 6)
    field = gaussian(keys[0], (SAMPLES, G, G, G * C), 1.0, 6.0, ((0, 16), (1, 8)))
    cotangent = gaussian(keys[1], (SAMPLES, G, G, G * C), 1.0, 6.0, ((0, 16), (1, 8)))
    spectral_weight = gaussian(keys[2], (K * K, K, C, 2 * C), (2 * C) ** -0.5, 0.5, ((0, 16), (1, 8)))
    point_weight = gaussian(keys[3], (C, C), C ** -0.5, 0.75)
    bias = gaussian(keys[4], (C,), 0.5, 3.0, (), jnp.float32)
    return dict(field=field, cotangent=cotangent, spectral_weight=spectral_weight, point_weight=point_weight, bias=bias)


def spectral_tables(length, modes):
    cells = jnp.arange(length, dtype=jnp.int32)
    index = jnp.arange(modes, dtype=jnp.int32)
    signed = jnp.where(index < modes // 2, index, index - modes)
    factor = 1.0 / math.sqrt(length)

    def angle(freq):
        turns = cells[:, None] * freq[None, :] % length
        return 2.0 * math.pi / length * turns.astype(jnp.float32)
    plain_angle = angle(index)
    real_table = jnp.stack([jnp.cos(plain_angle) * factor, -jnp.sin(plain_angle) * factor], axis=1)
    doubling = jnp.where(index == 0, 1.0, 2.0).astype(jnp.float32)
    weighted = real_table * doubling[None, None, :]
    signed_angle = angle(signed)
    cosine = jnp.cos(signed_angle) * factor
    sine = -jnp.sin(signed_angle) * factor
    complex_table = jnp.stack([jnp.stack([cosine, sine], axis=1), jnp.stack([-sine, cosine], axis=1)], axis=1)
    return (real_table.astype(jnp.bfloat16), weighted.astype(jnp.bfloat16), complex_table.astype(jnp.bfloat16))

def widen(weight):
    real_part = weight[..., :C]
    imag_part = weight[..., C:]
    lower = jnp.concatenate([-imag_part, real_part], axis=-1)
    return jnp.concatenate([weight, lower], axis=-2)

def gelu_slope(values):
    normal_cdf = 0.5 * (1.0 + jax.scipy.special.erf(values * 0.7071067811865476))
    density = jnp.exp(-0.5 * values * values) * 0.3989422804014327
    return normal_cdf + values * density

def reference(field, cotangent, spectral_weight, point_weight, bias):
    real_table, weighted, complex_table = spectral_tables(G, K)
    plain_f = real_table.astype(jnp.float32)
    weighted_f = weighted.astype(jnp.float32)
    table_f = complex_table.astype(jnp.float32)
    point_f = point_weight.astype(jnp.float32)

    def forward_one(sample, table):
        volume = sample.reshape(G, G, G, C).astype(jnp.float32)
        first = jnp.einsum('pyxc,xrk->pyrkc', volume, table).astype(jnp.bfloat16)
        second = jnp.einsum('pyrkc,yrqj->pjqkc', first.astype(jnp.float32), table_f).astype(jnp.bfloat16)
        third = jnp.einsum('xjrkc,xrqi->ikjqc', second.astype(jnp.float32), table_f).astype(jnp.bfloat16)
        return third.reshape(K * K, K, 2 * C)

    def grid_one(spectrum, table):
        waves = spectrum.reshape(K, K, K, 2, C).astype(jnp.float32)
        first = jnp.einsum('ikjqo,xrqi->xjrko', waves, table_f).astype(jnp.bfloat16)
        second = jnp.einsum('xjqko,yrqj->xyrko', first.astype(jnp.float32), table_f).astype(jnp.bfloat16)
        return jnp.einsum('xyrko,zrk->xyzo', second.astype(jnp.float32), table)

    def forward_plain(sample):
        return forward_one(sample, plain_f)
    field_modes = lax.map(forward_plain, field)
    wide = widen(spectral_weight).astype(jnp.float32)
    mixed = jnp.einsum('smja,mjab->smjb', field_modes.astype(jnp.float32), wide).astype(jnp.bfloat16)

    def middle(items):
        sample, upstream, mixed_one = items
        volume = sample.reshape(G, G, G, C).astype(jnp.float32)
        pre = jnp.einsum('pyxc,cd->pyxd', volume, point_f) + bias + grid_one(mixed_one, weighted_f)
        slope = gelu_slope(pre)
        pre_grad = (upstream.reshape(G, G, G, C).astype(jnp.float32) * slope).astype(jnp.bfloat16)
        return (pre_grad, forward_one(pre_grad.reshape(G, G, G * C), weighted_f))
    pre_grad, grad_modes = lax.map(middle, (field, cotangent, mixed))
    modes_f = field_modes.astype(jnp.float32)
    grads_f = grad_modes.astype(jnp.float32)
    real_u = modes_f[..., :C]
    imag_u = modes_f[..., C:]
    swapped = jnp.concatenate([grads_f[..., C:], -grads_f[..., :C]], axis=-1)
    weight_grad = jnp.einsum('smjc,smjo->mjco', real_u, grads_f) + jnp.einsum('smjc,smjo->mjco', imag_u, swapped)
    weight_grad = weight_grad / SAMPLES
    modes_grad = jnp.einsum('smjb,mjab->smja', grads_f, wide).astype(jnp.bfloat16)

    def finish(items):
        pre_one, modes_one = items
        local = jnp.einsum('pyxd,cd->pyxc', pre_one.astype(jnp.float32), point_f)
        total = local + grid_one(modes_one, plain_f)
        return total.astype(jnp.bfloat16).reshape(G, G, G * C)
    field_grad = lax.map(finish, (pre_grad, modes_grad))
    return (field_grad, weight_grad)
```

```python
import math

import jax
import jax.numpy as jnp
import ml_dtypes
import numpy as np
from jax import lax
from jax.experimental import pallas as pl
from jax.experimental.pallas import tpu as pltpu
from jax.sharding import PartitionSpec as P

C = 64
K = 16
G = 64
H = G // 2
LANES = 2 * C
PLANES = 8
PAIRS = PLANES // 2
SPACE = 8
DP = 16
HERE = 2
SAMPLES = 32
F32 = jnp.float32
BF16 = jnp.bfloat16


def cosine(turns):
    return np.cos(2.0 * np.pi * (turns % G) / G)


def sine(turns):
    return np.sin(2.0 * np.pi * (turns % G) / G)


def grid_table():
    freq = np.arange(K)
    signed = np.where(freq < K // 2, freq, freq - K)
    turns = (
        signed[:, None, None, None] * np.arange(G)[None, None, None, :]
        + freq[None, :, None, None] * 2 * np.arange(H)[None, None, :, None]
    )
    table = np.stack([cosine(turns), -sine(turns)], axis=1) / G
    return table.reshape(2 * K * K, G * H)


def plane_table():
    freq = np.arange(K)
    signed = np.where(freq < K // 2, freq, freq - K)
    planes = PLANES * np.arange(SPACE)[:, None] + 2 * np.arange(PAIRS)[None, :]
    turns = signed[:, None, None] * planes[None]
    cos, sin = cosine(turns) / 8.0, sine(turns) / 8.0
    table = np.zeros((2, 2, K, SPACE, 2, 2, PAIRS))
    for j in range(2):
        table[j, 0, :, :, j, 0] = cos
        table[j, 0, :, :, j, 1] = sin
        table[j, 1, :, :, j, 0] = -sin
        table[j, 1, :, :, j, 1] = cos
    return table.reshape(4 * K, SPACE * 16)


def plane_inverse_table():
    freq = np.arange(K)
    signed = np.where(freq < K // 2, freq, freq - K)
    turns = (PLANES * np.arange(SPACE)[:, None, None] + np.arange(PLANES)[None, :, None]) * signed
    cos, sin = cosine(turns) / 8.0, sine(turns) / 8.0
    table = np.zeros((SPACE, 2, PLANES, 2, K))
    table[:, 0, :, 0] = cos
    table[:, 0, :, 1] = -sin
    table[:, 1, :, 0] = sin
    table[:, 1, :, 1] = cos
    return table.reshape(SPACE * 2 * PLANES, 2 * K)


def cell_factor(weighted):
    freq = np.arange(K)
    weight = np.where(freq == 0, 1.0, 2.0) if weighted else np.ones(K)
    out = np.zeros((2, K, 2, C))
    out[0, :, 0] = weight[:, None]
    out[0, :, 1] = (weight * cosine(freq))[:, None]
    out[1, :, 1] = (weight * sine(freq))[:, None]
    return out.reshape(2, K, LANES).astype(np.float32)


def plane_factor():
    freq = np.arange(K)
    signed = np.where(freq < K // 2, freq, freq - K)
    out = np.zeros((2, K, 2, C))
    out[0, :, 0] = 1.0
    out[0, :, 1] = cosine(signed)[:, None]
    out[1, :, 1] = sine(signed)[:, None]
    return out.reshape(2, K, LANES).astype(np.float32)


def bf16_table(values):
    return np.asarray(values, np.float32).astype(ml_dtypes.bfloat16)


def low_lanes(rows):
    return lax.broadcasted_iota(jnp.int32, (rows, LANES), 1) < C


def swap_halves(tile):
    return pltpu.roll(tile, C, 1)


def fold_halves(low, first, second):
    return jnp.where(low, first, second) + swap_halves(jnp.where(low, second, first))


def pair_operand(first, second):
    parts = []
    for h in range(H):
        lanes = slice(h * LANES, (h + 1) * LANES)
        parts.append(jnp.concatenate([first[:, lanes], second[:, lanes]], axis=1))
    return jnp.concatenate(parts, axis=0)


def forward_pair(table_ref, factor_ref, operand, scratch, pair):
    modes = jnp.dot(table_ref[...], operand, preferred_element_type=F32)
    low = low_lanes(K)
    cos, sin = factor_ref[0], factor_ref[1]
    for j2 in range(K):
        halves = ([], [])
        for plane in range(2):
            lanes = slice(plane * LANES, (plane + 1) * LANES)
            real = modes[j2 * 32 : j2 * 32 + K, lanes]
            imag = modes[j2 * 32 + K : j2 * 32 + 2 * K, lanes]
            halves[0].append(real * cos + imag * sin)
            halves[1].append(imag * cos - real * sin)
        for q in range(2):
            start = (j2 // 2) * 256 + (j2 % 2) * 8 + q * PAIRS + pair
            scratch[pl.ds(start, K, stride=16), :] = fold_halves(low, *halves[q])


def store_forward(scratch, out_ref):
    for p in range(SPACE):
        out_ref[p, 0] = scratch[p * 256 : (p + 1) * 256, :].reshape(K, 16, LANES).astype(BF16)


def forward_kernel(field_ref, table_ref, factor_ref, out_ref, scratch):
    pair = pl.program_id(1)
    operand = pair_operand(field_ref[0, 0], field_ref[0, 1])
    forward_pair(table_ref, factor_ref, operand, scratch, pair)

    @pl.when(pair == PAIRS - 1)
    def _():
        store_forward(scratch, out_ref)


def to_weights_kernel(arrived_ref, table_ref, factor_ref, out_ref, scratch):
    low = low_lanes(K)
    cos, sin = factor_ref[0], factor_ref[1]
    for s in range(HERE):
        operand = jnp.concatenate(
            [
                jnp.concatenate([arrived_ref[w, s, k3] for w in range(SPACE)], axis=0)
                for k3 in range(K)
            ],
            axis=1,
        )
        modes = jnp.dot(table_ref[...], operand, preferred_element_type=F32)
        for k3 in range(K):
            lanes = slice(k3 * LANES, (k3 + 1) * LANES)
            for j in range(2):
                real = modes[j * 32 : j * 32 + K, lanes]
                imag = modes[j * 32 + K : j * 32 + 2 * K, lanes]
                scratch[pl.ds(s * 32 + k3 * 2 + j, K, stride=64), :] = fold_halves(
                    low, real * cos + imag * sin, imag * cos - real * sin
                )
    out_ref[...] = scratch[...].reshape(DP, 64, LANES).astype(BF16)


def wide_of(weight_ref, item, low):
    top = weight_ref[item // 2, item % 2].astype(F32)
    turned = swap_halves(top)
    return jnp.concatenate([top, jnp.where(low, -turned, turned)], axis=0).astype(BF16)


def gather_rows(modes_ref, scratch):
    scratch[...] = modes_ref[...].reshape(DP * 64, LANES).astype(F32)


def mix_kernel(modes_ref, weight_ref, out_ref, scratch, mixed):
    low = low_lanes(C)
    gather_rows(modes_ref, scratch)
    for item in range(32):
        rows = scratch[pl.ds(item, SAMPLES, stride=32), :].astype(BF16)
        mixed[pl.ds(item, SAMPLES, stride=32), :] = jnp.dot(
            rows, wide_of(weight_ref, item, low), preferred_element_type=F32
        )
    out_ref[...] = mixed[...].reshape(DP, 64, LANES).astype(BF16)


def mix_back_kernel(
    field_modes_ref, grad_modes_ref, weight_ref, out_ref, weight_grad_ref, scratch, scratch_u, mixed
):
    low = low_lanes(C)
    gather_rows(grad_modes_ref, scratch)
    gather_rows(field_modes_ref, scratch_u)
    for item in range(32):
        rows = scratch[pl.ds(item, SAMPLES, stride=32), :].astype(BF16)
        field_rows = scratch_u[pl.ds(item, SAMPLES, stride=32), :].astype(BF16)
        mixed[pl.ds(item, SAMPLES, stride=32), :] = lax.dot_general(
            rows, wide_of(weight_ref, item, low), (((1,), (1,)), ((), ())), preferred_element_type=F32
        )
        outer = lax.dot_general(
            field_rows, rows, (((0,), (0,)), ((), ())), preferred_element_type=F32
        )
        turned = swap_halves(outer[C:])
        weight_grad_ref[item // 2, item % 2] = (
            outer[:C] + jnp.where(low, turned, -turned)
        ) * (1.0 / SAMPLES)
    out_ref[...] = mixed[...].reshape(DP, 64, LANES).astype(BF16)


def to_planes_kernel(mixed_ref, table_ref, out_ref, scratch, planes):
    low = low_lanes(K)
    scratch[...] = mixed_ref[...].reshape(DP * 64, LANES).astype(F32)
    for s in range(HERE):
        columns = []
        for k3 in range(K):
            first = scratch[pl.ds(s * 32 + k3 * 2, K, stride=64), :]
            second = scratch[pl.ds(s * 32 + k3 * 2 + 1, K, stride=64), :]
            real = jnp.where(low, first, swap_halves(second))
            imag = jnp.where(low, swap_halves(first), second)
            columns.append(jnp.concatenate([real, imag], axis=0).astype(BF16))
        partial = jnp.dot(
            table_ref[...], jnp.concatenate(columns, axis=1), preferred_element_type=F32
        )
        for p in range(SPACE):
            for r in range(2):
                row = (p * 2 + r) * PLANES
                for k3 in range(K):
                    planes[pl.ds(p * 256 + r * K + k3, PLANES, stride=32), :] = partial[
                        row : row + PLANES, k3 * LANES : (k3 + 1) * LANES
                    ]
            out_ref[p, s] = planes[p * 256 : (p + 1) * 256, :].reshape(PLANES, 32, LANES).astype(BF16)


def inverse_operand(arrived_ref, factor_ref):
    low = low_lanes(K)
    cos, sin = factor_ref[0], factor_ref[1]
    columns = []
    for plane in range(2):
        rows = []
        for w in range(SPACE):
            tile = arrived_ref[w, 0, plane].astype(F32)
            real, imag = tile[:K], tile[K:]
            real_turned, imag_turned = swap_halves(real), swap_halves(imag)
            for j in range(2):
                if j == 0:
                    re = jnp.where(low, real, real_turned)
                    im = jnp.where(low, imag, imag_turned)
                else:
                    re = jnp.where(low, real_turned, real)
                    im = jnp.where(low, imag_turned, imag)
                rows.append((re * cos - im * sin).astype(BF16))
                rows.append((im * cos + re * sin).astype(BF16))
        columns.append(jnp.concatenate(rows, axis=0))
    return jnp.concatenate(columns, axis=1)


def gelu_slope(values):
    normal_cdf = 0.5 * (1.0 + lax.erf(values * 0.7071067811865476))
    density = jnp.exp(-0.5 * values * values) * 0.3989422804014327
    return normal_cdf + values * density


def middle_kernel(
    arrived_ref,
    field_ref,
    cotangent_ref,
    inverse_ref,
    table_ref,
    factor_ref,
    point_ref,
    bias_ref,
    pre_grad_ref,
    out_ref,
    scratch,
    operand_ref,
):
    pair = pl.program_id(1)
    operand_ref[...] = inverse_operand(arrived_ref, factor_ref)
    bias = bias_ref[...]

    def step(block, carry):
        wide = 4 * LANES
        start = pl.multiple_of(block * wide, wide)
        spectral = jnp.dot(
            inverse_ref[pl.ds(pl.multiple_of(block * 256, 256), 256), :],
            operand_ref[...],
            preferred_element_type=F32,
        )
        for plane in range(2):
            cells = field_ref[0, plane, :, pl.ds(start, wide)]
            upstream = cotangent_ref[0, plane, :, pl.ds(start, wide)]
            for part in range(2):
                local = jnp.dot(
                    cells[:, part * 256 : (part + 1) * 256], point_ref[...], preferred_element_type=F32
                )
                for half in range(2):
                    h = part * 2 + half
                    pre = (
                        local[:, half * LANES : (half + 1) * LANES]
                        + bias
                        + spectral[h * G : (h + 1) * G, plane * LANES : (plane + 1) * LANES]
                    )
                    grad = upstream[:, h * LANES : (h + 1) * LANES].astype(F32) * gelu_slope(pre)
                    lanes = pl.ds(pl.multiple_of(start + h * LANES, LANES), LANES)
                    pre_grad_ref[0, plane, :, lanes] = grad.astype(BF16)
        return carry

    lax.fori_loop(0, H // 4, step, 0)
    operand = pair_operand(pre_grad_ref[0, 0], pre_grad_ref[0, 1])
    forward_pair(table_ref, factor_ref, operand, scratch, pair)

    @pl.when(pair == PAIRS - 1)
    def _():
        store_forward(scratch, out_ref)


def final_kernel(arrived_ref, pre_grad_ref, inverse_ref, factor_ref, point_ref, out_ref, operand_ref):
    operand_ref[...] = inverse_operand(arrived_ref, factor_ref)

    def step(block, carry):
        wide = 4 * LANES
        start = pl.multiple_of(block * wide, wide)
        spectral = jnp.dot(
            inverse_ref[pl.ds(pl.multiple_of(block * 256, 256), 256), :],
            operand_ref[...],
            preferred_element_type=F32,
        )
        for plane in range(2):
            cells = pre_grad_ref[0, plane, :, pl.ds(start, wide)]
            for part in range(2):
                local = jnp.dot(
                    cells[:, part * 256 : (part + 1) * 256], point_ref[...], preferred_element_type=F32
                )
                for half in range(2):
                    h = part * 2 + half
                    total = (
                        local[:, half * LANES : (half + 1) * LANES]
                        + spectral[h * G : (h + 1) * G, plane * LANES : (plane + 1) * LANES]
                    )
                    lanes = pl.ds(pl.multiple_of(start + h * LANES, LANES), LANES)
                    out_ref[0, plane, :, lanes] = total.astype(BF16)
        return carry

    lax.fori_loop(0, H // 4, step, 0)


def whole(shape):
    return pl.BlockSpec(shape, lambda s, pair: (0,) * len(shape))


def params(mib):
    return pltpu.CompilerParams(vmem_limit_bytes=mib * 1024 * 1024)


GRID_BLOCK = pl.BlockSpec((1, 2, G, G * C), lambda s, pair: (s, pair, 0, 0))
SENT_BLOCK = pl.BlockSpec((SPACE, 1, K, 16, LANES), lambda s, pair: (0, s, 0, 0, 0))
ARRIVED_BLOCK = pl.BlockSpec((SPACE, 1, 2, 32, LANES), lambda s, pair: (0, s, pair, 0, 0))
SENT = jax.ShapeDtypeStruct((SPACE, HERE, K, 16, LANES), BF16)
MODES = jax.ShapeDtypeStruct((DP, 64, LANES), BF16)
RETURNED = jax.ShapeDtypeStruct((SPACE, HERE, PLANES, 32, LANES), BF16)
ROWS_SCRATCH = pltpu.VMEM((DP * 64, LANES), F32)
SENT_SCRATCH = pltpu.VMEM((SPACE * 256, LANES), F32)


def on_device(field, cotangent, spectral_weight, point_weight, bias):
    table = grid_table()
    forward = jnp.asarray(bf16_table(table))
    inverse = jnp.asarray(bf16_table(table.T))
    to_modes = jnp.asarray(bf16_table(plane_table()))
    to_planes = jnp.asarray(bf16_table(plane_inverse_table()))
    plain = jnp.asarray(cell_factor(False))
    weighted = jnp.asarray(cell_factor(True))
    turn = jnp.asarray(plane_factor())
    eye = jnp.eye(4, dtype=BF16)
    point = jnp.kron(eye, point_weight)
    point_back = jnp.kron(eye, point_weight.T)
    bias_row = jnp.tile(bias, 2)[None, :]

    def space_exchange(sent):
        return lax.all_to_all(sent, "space", split_axis=0, concat_axis=0, tiled=True)

    def dp_exchange(sent):
        return lax.all_to_all(sent, "dp", split_axis=0, concat_axis=0, tiled=True)

    def to_weights(arrived):
        sent = pl.pallas_call(
            to_weights_kernel,
            out_shape=MODES,
            scratch_shapes=[ROWS_SCRATCH],
            compiler_params=params(16),
            name="to_weights",
        )(arrived, to_modes, turn)
        return dp_exchange(sent)

    def from_weights(mixed):
        sent = pl.pallas_call(
            to_planes_kernel,
            out_shape=RETURNED,
            scratch_shapes=[ROWS_SCRATCH, SENT_SCRATCH],
            compiler_params=params(16),
            name="to_planes",
        )(dp_exchange(mixed), to_planes)
        return space_exchange(sent)

    sent = pl.pallas_call(
        forward_kernel,
        grid=(HERE, PAIRS),
        in_specs=[GRID_BLOCK, whole(forward.shape), whole(plain.shape)],
        out_specs=SENT_BLOCK,
        out_shape=SENT,
        scratch_shapes=[SENT_SCRATCH],
        compiler_params=params(32),
        name="forward",
    )(field, forward, plain)
    field_modes = to_weights(space_exchange(sent))
    mixed = pl.pallas_call(
        mix_kernel,
        out_shape=MODES,
        scratch_shapes=[ROWS_SCRATCH, ROWS_SCRATCH],
        compiler_params=params(16),
        name="mix",
    )(field_modes, spectral_weight)
    arrived = from_weights(mixed)
    pre_grad, sent = pl.pallas_call(
        middle_kernel,
        grid=(HERE, PAIRS),
        in_specs=[
            ARRIVED_BLOCK,
            GRID_BLOCK,
            GRID_BLOCK,
            whole(inverse.shape),
            whole(forward.shape),
            whole(weighted.shape),
            whole(point.shape),
            whole(bias_row.shape),
        ],
        out_specs=[GRID_BLOCK, SENT_BLOCK],
        out_shape=[jax.ShapeDtypeStruct(field.shape, BF16), SENT],
        scratch_shapes=[SENT_SCRATCH, pltpu.VMEM((2 * K * K, 2 * LANES), BF16)],
        compiler_params=params(40),
        name="middle",
    )(arrived, field, cotangent, inverse, forward, weighted, point, bias_row)
    grad_modes = to_weights(space_exchange(sent))
    modes_grad, weight_grad = pl.pallas_call(
        mix_back_kernel,
        out_shape=[MODES, jax.ShapeDtypeStruct(spectral_weight.shape, F32)],
        scratch_shapes=[ROWS_SCRATCH, ROWS_SCRATCH, ROWS_SCRATCH],
        compiler_params=params(16),
        name="mix_back",
    )(field_modes, grad_modes, spectral_weight)
    arrived = from_weights(modes_grad)
    field_grad = pl.pallas_call(
        final_kernel,
        grid=(HERE, PAIRS),
        in_specs=[
            ARRIVED_BLOCK,
            GRID_BLOCK,
            whole(inverse.shape),
            whole(plain.shape),
            whole(point_back.shape),
        ],
        out_specs=GRID_BLOCK,
        out_shape=jax.ShapeDtypeStruct(field.shape, BF16),
        scratch_shapes=[pltpu.VMEM((2 * K * K, 2 * LANES), BF16)],
        compiler_params=params(32),
        name="final",
    )(arrived, pre_grad, inverse, plain, point_back)
    return (field_grad, weight_grad)


def solution(mesh):
    return jax.shard_map(
        on_device,
        mesh=mesh,
        in_specs=(
            P("dp", "space", None, None),
            P("dp", "space", None, None),
            P("dp", "space", None, None),
            P(),
            P(),
        ),
        out_specs=(P("dp", "space", None, None), P("dp", "space", None, None)),
        check_vma=False,
    )
```

```python
import functools

import jax
import jax.numpy as jnp
import ml_dtypes
import numpy as np
from jax import lax
from jax.experimental import pallas as pl
from jax.experimental.pallas import tpu as pltpu
from jax.sharding import PartitionSpec as P

C = 64
K = 16
G = 64
H = G // 2
LANES = 2 * C
PLANES = 8
PAIRS = PLANES // 2
SPACE = 8
DP = 16
HERE = 2
SAMPLES = 32
F32 = jnp.float32
BF16 = jnp.bfloat16


def cosine(turns):
    return np.cos(2.0 * np.pi * (turns % G) / G)


def sine(turns):
    return np.sin(2.0 * np.pi * (turns % G) / G)


def grid_table():
    freq = np.arange(K)
    signed = np.where(freq < K // 2, freq, freq - K)
    k3 = freq.reshape(K // 2, 2).T
    turns = (
        signed[None, :, None, None, None] * np.arange(G)
        + k3[:, None, :, None, None] * 2 * np.arange(H // 2)[:, None]
    )
    table = np.stack([cosine(turns), -sine(turns)], axis=2) / G
    return table.reshape(2, K * K, G * H // 2)


def plane_table():
    freq = np.arange(K)
    signed = np.where(freq < K // 2, freq, freq - K)
    planes = PLANES * np.arange(SPACE)[:, None] + 2 * np.arange(PAIRS)[None, :]
    turns = signed[:, None, None] * planes[None]
    cos, sin = cosine(turns) / 8.0, sine(turns) / 8.0
    table = np.zeros((2, 2, K, SPACE, 2, 2, PAIRS))
    for j in range(2):
        table[j, 0, :, :, j, 0] = cos
        table[j, 0, :, :, j, 1] = sin
        table[j, 1, :, :, j, 0] = -sin
        table[j, 1, :, :, j, 1] = cos
    return table.reshape(4 * K, SPACE * 16)


def plane_inverse_table():
    freq = np.arange(K)
    signed = np.where(freq < K // 2, freq, freq - K)
    turns = (PLANES * np.arange(SPACE)[:, None, None] + np.arange(PLANES)[None, :, None]) * signed
    cos, sin = cosine(turns) / 8.0, sine(turns) / 8.0
    table = np.zeros((SPACE, 2, PLANES, 2, K))
    table[:, 0, :, 0] = cos
    table[:, 0, :, 1] = -sin
    table[:, 1, :, 0] = sin
    table[:, 1, :, 1] = cos
    return table.reshape(SPACE * 2 * PLANES, 2 * K)


def cell_factor(weighted):
    freq = np.arange(K)
    weight = np.where(freq == 0, 1.0, 2.0) if weighted else np.ones(K)
    out = np.zeros((2, K, 2, C))
    out[0, :, 0] = weight[:, None]
    out[0, :, 1] = (weight * cosine(freq))[:, None]
    out[1, :, 1] = (weight * sine(freq))[:, None]
    out = out.reshape(2, K // 2, 2, LANES).transpose(2, 0, 1, 3)
    return np.ascontiguousarray(out, dtype=np.float32)


def plane_factor():
    freq = np.arange(K)
    signed = np.where(freq < K // 2, freq, freq - K)
    out = np.zeros((2, K, 2, C))
    out[0, :, 0] = 1.0
    out[0, :, 1] = cosine(signed)[:, None]
    out[1, :, 1] = sine(signed)[:, None]
    return out.reshape(2, K, LANES).astype(np.float32)


def bf16_table(values):
    return np.asarray(values, np.float32).astype(ml_dtypes.bfloat16)


def low_lanes(rows):
    return lax.broadcasted_iota(jnp.int32, (rows, LANES), 1) < C


def swap_halves(tile):
    return pltpu.roll(tile, C, 1)


def fold_halves(low, first, second):
    return jnp.where(low, first, second) + swap_halves(jnp.where(low, second, first))


def cell_tiles(planes, h):
    lanes = slice(h * LANES, (h + 1) * LANES)
    return jnp.concatenate([plane[:, lanes] for plane in planes], axis=1)


def forward_pair(table_ref, factor_ref, planes, scratch, pair):
    low = low_lanes(K // 2)
    for b in range(2):
        parts = []
        for h in range(H // 2):
            near, far = cell_tiles(planes, h), cell_tiles(planes, h + H // 2)
            parts.append(near - far if b else near + far)
        modes = jnp.dot(
            table_ref[b], jnp.concatenate(parts, axis=0), preferred_element_type=F32
        )
        cos, sin = factor_ref[b, 0], factor_ref[b, 1]
        for j2 in range(K):
            halves = ([], [])
            for plane in range(2):
                lanes = slice(plane * LANES, (plane + 1) * LANES)
                real = modes[j2 * K : j2 * K + 8, lanes]
                imag = modes[j2 * K + 8 : j2 * K + 16, lanes]
                halves[0].append(real * cos + imag * sin)
                halves[1].append(imag * cos - real * sin)
            for q in range(2):
                start = (j2 // 2) * 256 + b * 16 + (j2 % 2) * 8 + q * PAIRS + pair
                scratch[pl.ds(start, 8, stride=32), :] = fold_halves(low, *halves[q])


def store_forward(scratch, out_ref):
    for p in range(SPACE):
        out_ref[p, 0] = scratch[p * 256 : (p + 1) * 256, :].reshape(K, 16, LANES).astype(BF16)


def forward_kernel(field_ref, table_ref, factor_ref, out_ref, scratch):
    pair = pl.program_id(1)
    forward_pair(table_ref, factor_ref, (field_ref[0, 0], field_ref[0, 1]), scratch, pair)

    @pl.when(pair == PAIRS - 1)
    def _():
        store_forward(scratch, out_ref)


def modes_of_sample(s, arrived, table_ref, factor_ref, rows, out):
    low = low_lanes(K)
    cos, sin = factor_ref[0], factor_ref[1]
    operand = jnp.concatenate(
        [
            jnp.concatenate([arrived[w, s, k3] for w in range(SPACE)], axis=0)
            for k3 in range(K)
        ],
        axis=1,
    )
    modes = jnp.dot(table_ref[...], operand, preferred_element_type=F32)
    for k3 in range(K):
        lanes = slice(k3 * LANES, (k3 + 1) * LANES)
        for j in range(2):
            real = modes[j * 32 : j * 32 + K, lanes]
            imag = modes[j * 32 + K : j * 32 + 2 * K, lanes]
            rows[pl.ds(k3 * 2 + j, K, stride=32), :] = fold_halves(
                low, real * cos + imag * sin, imag * cos - real * sin
            )
    out[s] = rows[...].reshape(DP, 32, LANES).astype(BF16)


def widen(weight_ref, wide):
    low = low_lanes(C)
    for item in range(32):
        top = weight_ref[item // 2, item % 2]
        turned = swap_halves(top.astype(F32))
        wide[item, :C] = top
        wide[item, C:] = jnp.where(low, -turned, turned).astype(BF16)


def mix_sample(s, backward, modes, wide, rows, mixed_rows, out):
    rows[...] = modes[s].reshape(DP * 32, LANES).astype(F32)
    dims = (((1,), (1,)), ((), ())) if backward else (((1,), (0,)), ((), ()))
    for item in range(32):
        here = pl.ds(item, DP, stride=32)
        mixed_rows[here, :] = lax.dot_general(
            rows[here, :].astype(BF16), wide[item], dims, preferred_element_type=F32
        )
    out[s] = mixed_rows[...].reshape(DP, 32, LANES).astype(BF16)


def weight_gradient(field_modes, grad_modes, rows, mixed_rows, weight_grad_ref):
    low = low_lanes(C)
    for s in range(HERE):
        rows[...] = field_modes[s].reshape(DP * 32, LANES).astype(F32)
        mixed_rows[...] = grad_modes[s].reshape(DP * 32, LANES).astype(F32)
        for item in range(32):
            here = pl.ds(item, DP, stride=32)
            outer = lax.dot_general(
                rows[here, :].astype(BF16),
                mixed_rows[here, :].astype(BF16),
                (((0,), (0,)), ((), ())),
                preferred_element_type=F32,
            )
            turned = swap_halves(outer[C:])
            term = (outer[:C] + jnp.where(low, turned, -turned)) * (1.0 / SAMPLES)
            if s == 0:
                weight_grad_ref[item // 2, item % 2] = term
            else:
                weight_grad_ref[item // 2, item % 2] += term


def planes_of_sample(s, mixed, table_ref, rows, planes, out):
    low = low_lanes(K)
    rows[...] = mixed[s].reshape(DP * 32, LANES).astype(F32)
    columns = []
    for k3 in range(K):
        first = rows[pl.ds(k3 * 2, K, stride=32), :]
        second = rows[pl.ds(k3 * 2 + 1, K, stride=32), :]
        real = jnp.where(low, first, swap_halves(second))
        imag = jnp.where(low, swap_halves(first), second)
        columns.append(jnp.concatenate([real, imag], axis=0).astype(BF16))
    partial = jnp.dot(
        table_ref[...], jnp.concatenate(columns, axis=1), preferred_element_type=F32
    )
    for p in range(SPACE):
        for r in range(2):
            row = (p * 2 + r) * PLANES
            for k3 in range(K):
                start = p * 256 + (k3 % 2) * 16 + r * 8 + k3 // 2
                planes[pl.ds(start, PLANES, stride=32), :] = partial[
                    row : row + PLANES, k3 * LANES : (k3 + 1) * LANES
                ]
        out[p, s] = planes[p * 256 : (p + 1) * 256, :].reshape(PLANES, 32, LANES).astype(BF16)


class Exchange:
    def __init__(self, axis, size, source, target, sems):
        self.axis, self.size, self.source, self.target = axis, size, source, target
        self.send, self.recv, self.own = sems
        self.me = lax.axis_index(axis)

    def remote(self, s, slot, peer):
        return pltpu.make_async_remote_copy(
            src_ref=self.source(peer, s),
            dst_ref=self.target(slot, s),
            send_sem=self.send.at[s, peer],
            recv_sem=self.recv.at[s, slot],
            device_id={self.axis: peer},
            device_id_type=pl.DeviceIdType.MESH,
        )

    def local(self, s):
        return pltpu.make_async_copy(
            self.source(self.me, s), self.target(self.me, s), self.own.at[s]
        )

    def peers(self, body):
        def step(offset, carry):
            body(lax.rem(self.me + offset, self.size))
            return carry

        lax.fori_loop(1, self.size, step, 0)

    def start(self, s):
        self.peers(lambda peer: self.remote(s, self.me, peer).start())
        self.local(s).start()

    def arrive(self, s):
        self.peers(lambda peer: self.remote(s, peer, peer).wait_recv())
        self.local(s).wait()

    def leave(self, s):
        self.peers(lambda peer: self.remote(s, self.me, peer).wait_send())


def meet():
    barrier = pltpu.get_barrier_semaphore()
    for axis, size in (("space", SPACE), ("dp", DP)):
        me = lax.axis_index(axis)

        def step(offset, carry):
            pl.semaphore_signal(
                barrier,
                inc=1,
                device_id={axis: lax.rem(me + offset, size)},
                device_id_type=pl.DeviceIdType.MESH,
            )
            return carry

        lax.fori_loop(1, size, step, 0)
    pl.semaphore_wait(barrier, SPACE + DP - 2)


def spectral_kernel(backward, *refs):
    if backward:
        sent, weight_ref, to_modes, to_planes, turn, field_modes, out, weight_grad = refs[:8]
    else:
        sent, weight_ref, to_modes, to_planes, turn, out, kept = refs[:7]
    sems = refs[-12:]
    arrived, modes_out, modes_in, mixed_out, mixed_in, planes_out, wide, rows, mixed_rows, planes = refs[-22:-12]
    by_space = lambda ref: lambda peer, s: ref.at[peer, s]
    by_dp = lambda ref: lambda peer, s: ref.at[s, peer]
    first = Exchange("space", SPACE, by_space(sent), by_space(arrived), sems[0:3])
    second = Exchange("dp", DP, by_dp(modes_out), by_dp(modes_in), sems[3:6])
    third = Exchange("dp", DP, by_dp(mixed_out), by_dp(mixed_in), sems[6:9])
    fourth = Exchange("space", SPACE, by_space(planes_out), by_space(out), sems[9:12])
    both = range(HERE)
    meet()
    for s in both:
        first.start(s)
    widen(weight_ref, wide)
    for s in both:
        first.arrive(s)
        modes_of_sample(s, arrived, to_modes, turn, rows, modes_out)
        second.start(s)
    for s in both:
        second.arrive(s)
        mix_sample(s, backward, modes_in, wide, rows, mixed_rows, mixed_out)
        third.start(s)
    for s in both:
        third.arrive(s)
        planes_of_sample(s, mixed_in, to_planes, rows, planes, planes_out)
        fourth.start(s)
    if backward:
        weight_gradient(field_modes, modes_in, rows, mixed_rows, weight_grad)
    else:
        kept[...] = modes_in[...]
    for s in both:
        for exchange in (first, second, third):
            exchange.leave(s)
    for s in both:
        fourth.arrive(s)
        fourth.leave(s)


def inverse_operand(arrived_ref, factor_ref, operand_ref):
    low = low_lanes(8)
    for plane in range(2):
        for b in range(2):
            cos, sin = factor_ref[b, 0], factor_ref[b, 1]
            for w in range(SPACE):
                tile = arrived_ref[w, 0, plane, b * 16 : (b + 1) * 16].astype(F32)
                real, imag = tile[:8], tile[8:]
                real_turned, imag_turned = swap_halves(real), swap_halves(imag)
                for j in range(2):
                    if j == 0:
                        re = jnp.where(low, real, real_turned)
                        im = jnp.where(low, imag, imag_turned)
                    else:
                        re = jnp.where(low, real_turned, real)
                        im = jnp.where(low, imag_turned, imag)
                    waves = jnp.concatenate([re * cos - im * sin, im * cos + re * sin], axis=0)
                    row = (2 * w + j) * 16
                    operand_ref[b, row : row + 16, plane * LANES : (plane + 1) * LANES] = waves.astype(BF16)


def on_cells(cells_ref, inverse_ref, operand_ref, point_ref, body):
    depth = 4
    for block in range(H // 2 // depth):
        rows = slice(block * depth * G, (block + 1) * depth * G)
        even = jnp.dot(inverse_ref[0, rows], operand_ref[0], preferred_element_type=F32)
        odd = jnp.dot(inverse_ref[1, rows], operand_ref[1], preferred_element_type=F32)
        for side in range(2):
            first = block * depth + side * (H // 2)
            planes = (cells_ref[0, 0], cells_ref[0, 1])
            cells = jnp.concatenate([cell_tiles(planes, first + i) for i in range(depth)], axis=0)
            local = jnp.dot(cells, point_ref[...], preferred_element_type=F32)
            total = local + (even - odd if side else even + odd)
            for i in range(depth):
                for plane in range(2):
                    body(
                        plane,
                        first + i,
                        total[i * G : (i + 1) * G, plane * LANES : (plane + 1) * LANES],
                    )


def gelu_slope(values):
    normal_cdf = 0.5 * (1.0 + lax.erf(values * 0.7071067811865476))
    density = jnp.exp(-0.5 * values * values) * 0.3989422804014327
    return normal_cdf + values * density


def middle_kernel(
    arrived_ref,
    field_ref,
    cotangent_ref,
    inverse_ref,
    table_ref,
    factor_ref,
    point_ref,
    bias_ref,
    pre_grad_ref,
    out_ref,
    scratch,
    operand_ref,
):
    pair = pl.program_id(1)
    inverse_operand(arrived_ref, factor_ref, operand_ref)
    bias = bias_ref[...]

    def body(plane, h, value):
        lanes = slice(h * LANES, (h + 1) * LANES)
        upstream = cotangent_ref[0, plane, :, lanes].astype(F32)
        pre_grad_ref[0, plane, :, lanes] = (upstream * gelu_slope(value + bias)).astype(BF16)

    on_cells(field_ref, inverse_ref, operand_ref, point_ref, body)
    forward_pair(table_ref, factor_ref, (pre_grad_ref[0, 0], pre_grad_ref[0, 1]), scratch, pair)

    @pl.when(pair == PAIRS - 1)
    def _():
        store_forward(scratch, out_ref)


def final_kernel(arrived_ref, pre_grad_ref, inverse_ref, factor_ref, point_ref, out_ref, operand_ref):
    inverse_operand(arrived_ref, factor_ref, operand_ref)

    def body(plane, h, value):
        out_ref[0, plane, :, h * LANES : (h + 1) * LANES] = value.astype(BF16)

    on_cells(pre_grad_ref, inverse_ref, operand_ref, point_ref, body)


def whole(shape):
    return pl.BlockSpec(shape, lambda s, pair: (0,) * len(shape))


def params(mib):
    return pltpu.CompilerParams(vmem_limit_bytes=mib * 1024 * 1024)


GRID_BLOCK = pl.BlockSpec((1, 2, G, G * C), lambda s, pair: (s, pair, 0, 0))
SENT_BLOCK = pl.BlockSpec((SPACE, 1, K, 16, LANES), lambda s, pair: (0, s, 0, 0, 0))
ARRIVED_BLOCK = pl.BlockSpec((SPACE, 1, 2, 32, LANES), lambda s, pair: (0, s, pair, 0, 0))
SENT = jax.ShapeDtypeStruct((SPACE, HERE, K, 16, LANES), BF16)
MODES = jax.ShapeDtypeStruct((HERE, DP, 32, LANES), BF16)
RETURNED = jax.ShapeDtypeStruct((SPACE, HERE, PLANES, 32, LANES), BF16)
ROWS_SCRATCH = pltpu.VMEM((DP * 32, LANES), F32)
OPERAND_SCRATCH = pltpu.VMEM((2, K * K, 2 * LANES), BF16)
ANYWHERE = pl.BlockSpec(memory_space=pl.ANY)
IN_VMEM = pl.BlockSpec(memory_space=pltpu.VMEM)
SENT_SCRATCH = pltpu.VMEM((SPACE * 256, LANES), F32)


def on_device(field, cotangent, spectral_weight, point_weight, bias):
    table = grid_table()
    forward = jnp.asarray(bf16_table(table))
    inverse = jnp.asarray(bf16_table(table.transpose(0, 2, 1)))
    to_modes = jnp.asarray(bf16_table(plane_table()))
    to_planes = jnp.asarray(bf16_table(plane_inverse_table()))
    plain = jnp.asarray(cell_factor(False))
    weighted = jnp.asarray(cell_factor(True))
    turn = jnp.asarray(plane_factor())
    eye = jnp.eye(4, dtype=BF16)
    point = jnp.kron(eye, point_weight)
    point_back = jnp.kron(eye, point_weight.T)
    bias_row = jnp.tile(bias, 2)[None, :]

    def spectral(sent, field_modes=None):
        backward = field_modes is not None
        scratch = [pltpu.VMEM(SENT.shape, BF16)]
        scratch += [pltpu.VMEM(MODES.shape, BF16)] * 4
        scratch += [
            pltpu.VMEM(RETURNED.shape, BF16),
            pltpu.VMEM((32, LANES, LANES), BF16),
            ROWS_SCRATCH,
            ROWS_SCRATCH,
            SENT_SCRATCH,
        ]
        for size in (SPACE, DP, DP, SPACE):
            scratch += [
                pltpu.SemaphoreType.DMA((HERE, size)),
                pltpu.SemaphoreType.DMA((HERE, size)),
                pltpu.SemaphoreType.DMA((HERE,)),
            ]
        second = jax.ShapeDtypeStruct(spectral_weight.shape, F32) if backward else MODES
        operands = [sent, spectral_weight, to_modes, to_planes, turn]
        specs = [ANYWHERE] + [IN_VMEM] * 4
        if backward:
            operands.append(field_modes)
            specs.append(IN_VMEM)
        return pl.pallas_call(
            functools.partial(spectral_kernel, backward),
            in_specs=specs,
            out_specs=[ANYWHERE, IN_VMEM],
            out_shape=[RETURNED, second],
            scratch_shapes=scratch,
            compiler_params=pltpu.CompilerParams(
                vmem_limit_bytes=24 * 1024 * 1024,
                collective_id=1 if backward else 0,
                has_side_effects=True,
            ),
            name="spectral_back" if backward else "spectral",
        )(*operands)

    sent = pl.pallas_call(
        forward_kernel,
        grid=(HERE, PAIRS),
        in_specs=[GRID_BLOCK, whole(forward.shape), whole(plain.shape)],
        out_specs=SENT_BLOCK,
        out_shape=SENT,
        scratch_shapes=[SENT_SCRATCH],
        compiler_params=params(32),
        name="forward",
    )(field, forward, plain)
    arrived, field_modes = spectral(sent)
    pre_grad, sent = pl.pallas_call(
        middle_kernel,
        grid=(HERE, PAIRS),
        in_specs=[
            ARRIVED_BLOCK,
            GRID_BLOCK,
            GRID_BLOCK,
            whole(inverse.shape),
            whole(forward.shape),
            whole(weighted.shape),
            whole(point.shape),
            whole(bias_row.shape),
        ],
        out_specs=[GRID_BLOCK, SENT_BLOCK],
        out_shape=[jax.ShapeDtypeStruct(field.shape, BF16), SENT],
        scratch_shapes=[SENT_SCRATCH, OPERAND_SCRATCH],
        compiler_params=params(40),
        name="middle",
    )(arrived, field, cotangent, inverse, forward, weighted, point, bias_row)
    arrived, weight_grad = spectral(sent, field_modes)
    field_grad = pl.pallas_call(
        final_kernel,
        grid=(HERE, PAIRS),
        in_specs=[
            ARRIVED_BLOCK,
            GRID_BLOCK,
            whole(inverse.shape),
            whole(plain.shape),
            whole(point_back.shape),
        ],
        out_specs=GRID_BLOCK,
        out_shape=jax.ShapeDtypeStruct(field.shape, BF16),
        scratch_shapes=[OPERAND_SCRATCH],
        compiler_params=params(32),
        name="final",
    )(arrived, pre_grad, inverse, plain, point_back)
    return (field_grad, weight_grad)


def solution(mesh):
    return jax.shard_map(
        on_device,
        mesh=mesh,
        in_specs=(
            P("dp", "space", None, None),
            P("dp", "space", None, None),
            P("dp", "space", None, None),
            P(),
            P(),
        ),
        out_specs=(P("dp", "space", None, None), P("dp", "space", None, None)),
        check_vma=False,
    )
```

```python
import jax
import jax.numpy as jnp
import ml_dtypes
import numpy as np
from jax import lax
from jax.experimental import pallas as pl
from jax.experimental.pallas import tpu as pltpu
from jax.sharding import PartitionSpec as P

C = 64
K = 16
G = 64
H = G // 2
LANES = 2 * C
PLANES = 8
PAIRS = PLANES // 2
SPACE = 8
DP = 16
HERE = 2
SAMPLES = 32
F32 = jnp.float32
BF16 = jnp.bfloat16


def cosine(turns):
    return np.cos(2.0 * np.pi * (turns % G) / G)


def sine(turns):
    return np.sin(2.0 * np.pi * (turns % G) / G)


def grid_table():
    freq = np.arange(K)
    signed = np.where(freq < K // 2, freq, freq - K)
    k3 = freq.reshape(K // 2, 2).T
    turns = (
        signed[None, :, None, None, None] * np.arange(G)
        + k3[:, None, :, None, None] * 2 * np.arange(H // 2)[:, None]
    )
    table = np.stack([cosine(turns), -sine(turns)], axis=2) / G
    return table.reshape(2, K * K, G * H // 2)


def plane_table():
    freq = np.arange(K)
    signed = np.where(freq < K // 2, freq, freq - K)
    planes = PLANES * np.arange(SPACE)[:, None] + 2 * np.arange(PAIRS)[None, :]
    turns = signed[:, None, None] * planes[None]
    cos, sin = cosine(turns) / 8.0, sine(turns) / 8.0
    table = np.zeros((2, 2, K, SPACE, 2, 2, PAIRS))
    for j in range(2):
        table[j, 0, :, :, j, 0] = cos
        table[j, 0, :, :, j, 1] = sin
        table[j, 1, :, :, j, 0] = -sin
        table[j, 1, :, :, j, 1] = cos
    return table.reshape(4 * K, SPACE * 16)


def plane_inverse_table():
    freq = np.arange(K)
    signed = np.where(freq < K // 2, freq, freq - K)
    turns = (PLANES * np.arange(SPACE)[:, None, None] + np.arange(PLANES)[None, :, None]) * signed
    cos, sin = cosine(turns) / 8.0, sine(turns) / 8.0
    table = np.zeros((SPACE, 2, PLANES, 2, K))
    table[:, 0, :, 0] = cos
    table[:, 0, :, 1] = -sin
    table[:, 1, :, 0] = sin
    table[:, 1, :, 1] = cos
    return table.reshape(SPACE * 2 * PLANES, 2 * K)


def cell_factor(weighted):
    freq = np.arange(K)
    weight = np.where(freq == 0, 1.0, 2.0) if weighted else np.ones(K)
    out = np.zeros((2, K, 2, C))
    out[0, :, 0] = weight[:, None]
    out[0, :, 1] = (weight * cosine(freq))[:, None]
    out[1, :, 1] = (weight * sine(freq))[:, None]
    out = out.reshape(2, K // 2, 2, LANES).transpose(2, 0, 1, 3)
    return np.ascontiguousarray(out, dtype=np.float32)


def plane_factor():
    freq = np.arange(K)
    signed = np.where(freq < K // 2, freq, freq - K)
    out = np.zeros((2, K, 2, C))
    out[0, :, 0] = 1.0
    out[0, :, 1] = cosine(signed)[:, None]
    out[1, :, 1] = sine(signed)[:, None]
    return out.reshape(2, K, LANES).astype(np.float32)


def bf16_table(values):
    return np.asarray(values, np.float32).astype(ml_dtypes.bfloat16)


def low_lanes(rows):
    return lax.broadcasted_iota(jnp.int32, (rows, LANES), 1) < C


def swap_halves(tile):
    return pltpu.roll(tile, C, 1)


def fold_halves(low, first, second):
    return jnp.where(low, first, second) + swap_halves(jnp.where(low, second, first))


def cell_tiles(planes, h):
    lanes = slice(h * LANES, (h + 1) * LANES)
    return jnp.concatenate([plane[:, lanes] for plane in planes], axis=1)


def forward_pair(table_ref, factor_ref, planes, scratch, pair):
    low = low_lanes(K // 2)
    for b in range(2):
        parts = []
        for h in range(H // 2):
            near, far = cell_tiles(planes, h), cell_tiles(planes, h + H // 2)
            parts.append(near - far if b else near + far)
        modes = jnp.dot(
            table_ref[b], jnp.concatenate(parts, axis=0), preferred_element_type=F32
        )
        cos, sin = factor_ref[b, 0], factor_ref[b, 1]
        for j2 in range(K):
            halves = ([], [])
            for plane in range(2):
                lanes = slice(plane * LANES, (plane + 1) * LANES)
                real = modes[j2 * K : j2 * K + 8, lanes]
                imag = modes[j2 * K + 8 : j2 * K + 16, lanes]
                halves[0].append(real * cos + imag * sin)
                halves[1].append(imag * cos - real * sin)
            for q in range(2):
                start = (j2 // 2) * 256 + b * 16 + (j2 % 2) * 8 + q * PAIRS + pair
                scratch[pl.ds(start, 8, stride=32), :] = fold_halves(low, *halves[q])


def store_forward(scratch, out, s):
    for p in range(SPACE):
        out[p, s] = scratch[p * 256 : (p + 1) * 256, :].reshape(K, 16, LANES).astype(BF16)


def modes_of_sample(s, arrived, table_ref, factor_ref, rows, out):
    low = low_lanes(K)
    cos, sin = factor_ref[0], factor_ref[1]
    operand = jnp.concatenate(
        [
            jnp.concatenate([arrived[w, s, k3] for w in range(SPACE)], axis=0)
            for k3 in range(K)
        ],
        axis=1,
    )
    modes = jnp.dot(table_ref[...], operand, preferred_element_type=F32)
    for k3 in range(K):
        lanes = slice(k3 * LANES, (k3 + 1) * LANES)
        for j in range(2):
            real = modes[j * 32 : j * 32 + K, lanes]
            imag = modes[j * 32 + K : j * 32 + 2 * K, lanes]
            rows[pl.ds(k3 * 2 + j, K, stride=32), :] = fold_halves(
                low, real * cos + imag * sin, imag * cos - real * sin
            )
    out[s] = rows[...].reshape(DP, 32, LANES).astype(BF16)


def widen(weight_ref, wide):
    low = low_lanes(C)
    for item in range(32):
        top = weight_ref[item // 2, item % 2]
        turned = swap_halves(top.astype(F32))
        wide[item, :C] = top
        wide[item, C:] = jnp.where(low, -turned, turned).astype(BF16)


def mix_sample(s, backward, modes, wide, rows, mixed_rows, out):
    rows[...] = modes[s].reshape(DP * 32, LANES).astype(F32)
    dims = (((1,), (1,)), ((), ())) if backward else (((1,), (0,)), ((), ()))
    for item in range(32):
        here = pl.ds(item, DP, stride=32)
        mixed_rows[here, :] = lax.dot_general(
            rows[here, :].astype(BF16), wide[item], dims, preferred_element_type=F32
        )
    out[s] = mixed_rows[...].reshape(DP, 32, LANES).astype(BF16)


def weight_gradient(field_modes, grad_modes, rows, mixed_rows, weight_grad_ref):
    low = low_lanes(C)
    for s in range(HERE):
        rows[...] = field_modes[s].reshape(DP * 32, LANES).astype(F32)
        mixed_rows[...] = grad_modes[s].reshape(DP * 32, LANES).astype(F32)
        for item in range(32):
            here = pl.ds(item, DP, stride=32)
            outer = lax.dot_general(
                rows[here, :].astype(BF16),
                mixed_rows[here, :].astype(BF16),
                (((0,), (0,)), ((), ())),
                preferred_element_type=F32,
            )
            turned = swap_halves(outer[C:])
            term = (outer[:C] + jnp.where(low, turned, -turned)) * (1.0 / SAMPLES)
            if s == 0:
                weight_grad_ref[item // 2, item % 2] = term
            else:
                weight_grad_ref[item // 2, item % 2] += term


def planes_of_sample(s, mixed, table_ref, rows, planes, out):
    low = low_lanes(K)
    rows[...] = mixed[s].reshape(DP * 32, LANES).astype(F32)
    columns = []
    for k3 in range(K):
        first = rows[pl.ds(k3 * 2, K, stride=32), :]
        second = rows[pl.ds(k3 * 2 + 1, K, stride=32), :]
        real = jnp.where(low, first, swap_halves(second))
        imag = jnp.where(low, swap_halves(first), second)
        columns.append(jnp.concatenate([real, imag], axis=0).astype(BF16))
    partial = jnp.dot(
        table_ref[...], jnp.concatenate(columns, axis=1), preferred_element_type=F32
    )
    for p in range(SPACE):
        for r in range(2):
            row = (p * 2 + r) * PLANES
            for k3 in range(K):
                start = p * 256 + (k3 % 2) * 16 + r * 8 + k3 // 2
                planes[pl.ds(start, PLANES, stride=32), :] = partial[
                    row : row + PLANES, k3 * LANES : (k3 + 1) * LANES
                ]
        out[p, s] = planes[p * 256 : (p + 1) * 256, :].reshape(PLANES, 32, LANES).astype(BF16)


class Exchange:
    def __init__(self, axis, size, source, target, sems):
        self.axis, self.size, self.source, self.target = axis, size, source, target
        self.send, self.recv, self.own = sems
        self.me = lax.axis_index(axis)

    def remote(self, s, slot, peer):
        return pltpu.make_async_remote_copy(
            src_ref=self.source(peer, s),
            dst_ref=self.target(slot, s),
            send_sem=self.send.at[s, peer],
            recv_sem=self.recv.at[s, slot],
            device_id={self.axis: peer},
            device_id_type=pl.DeviceIdType.MESH,
        )

    def local(self, s):
        return pltpu.make_async_copy(
            self.source(self.me, s), self.target(self.me, s), self.own.at[s]
        )

    def peers(self, body):
        def step(offset, carry):
            body(lax.rem(self.me + offset, self.size))
            return carry

        lax.fori_loop(1, self.size, step, 0)

    def start(self, s):
        self.peers(lambda peer: self.remote(s, self.me, peer).start())
        self.local(s).start()

    def arrive(self, s):
        self.peers(lambda peer: self.remote(s, peer, peer).wait_recv())
        self.local(s).wait()

    def leave(self, s):
        self.peers(lambda peer: self.remote(s, self.me, peer).wait_send())


def greet():
    barrier = pltpu.get_barrier_semaphore()
    for axis, size in (("space", SPACE), ("dp", DP)):
        me = lax.axis_index(axis)

        def step(offset, carry):
            pl.semaphore_signal(
                barrier,
                inc=1,
                device_id={axis: lax.rem(me + offset, size)},
                device_id_type=pl.DeviceIdType.MESH,
            )
            return carry

        lax.fori_loop(1, size, step, 0)
    return barrier


def inverse_operand(tile_of, factor_ref, operand_ref):
    low = low_lanes(8)
    for plane in range(2):
        for b in range(2):
            cos, sin = factor_ref[b, 0], factor_ref[b, 1]
            for w in range(SPACE):
                tile = tile_of(w, plane, slice(b * 16, (b + 1) * 16)).astype(F32)
                real, imag = tile[:8], tile[8:]
                real_turned, imag_turned = swap_halves(real), swap_halves(imag)
                for j in range(2):
                    if j == 0:
                        re = jnp.where(low, real, real_turned)
                        im = jnp.where(low, imag, imag_turned)
                    else:
                        re = jnp.where(low, real_turned, real)
                        im = jnp.where(low, imag_turned, imag)
                    waves = jnp.concatenate([re * cos - im * sin, im * cos + re * sin], axis=0)
                    row = (2 * w + j) * 16
                    operand_ref[b, row : row + 16, plane * LANES : (plane + 1) * LANES] = waves.astype(BF16)


def on_cells(planes, inverse_ref, operand_ref, point_ref, back, body):
    depth = 4
    dims = (((1,), (1 if back else 0,)), ((), ()))
    for block in range(H // 2 // depth):
        rows = slice(block * depth * G, (block + 1) * depth * G)
        even = jnp.dot(inverse_ref[0, rows], operand_ref[0], preferred_element_type=F32)
        odd = jnp.dot(inverse_ref[1, rows], operand_ref[1], preferred_element_type=F32)
        for side in range(2):
            first = block * depth + side * (H // 2)
            cells = jnp.concatenate([cell_tiles(planes, first + i) for i in range(depth)], axis=0)
            local = lax.dot_general(cells, point_ref[...], dims, preferred_element_type=F32)
            total = local + (even - odd if side else even + odd)
            for i in range(depth):
                for plane in range(2):
                    body(
                        plane,
                        first + i,
                        total[i * G : (i + 1) * G, plane * LANES : (plane + 1) * LANES],
                    )


def gelu_slope(values):
    normal_cdf = 0.5 * (1.0 + lax.erf(values * 0.7071067811865476))
    density = jnp.exp(-0.5 * values * values) * 0.3989422804014327
    return normal_cdf + values * density


def spread_point(point_ref, point):
    low = low_lanes(C)
    twice = jnp.concatenate([point_ref[...], point_ref[...]], axis=1).astype(F32)
    none = jnp.zeros((LANES, LANES), BF16)
    both = jnp.concatenate(
        [jnp.where(low, twice, 0.0), jnp.where(low, 0.0, twice)], axis=0
    ).astype(BF16)
    point[:LANES, :LANES] = both
    point[:LANES, LANES:] = none
    point[LANES:, :LANES] = none
    point[LANES:, LANES:] = both


class Pass:
    def __init__(self, backward, buffers, final, sems, shared):
        self.backward, self.shared = backward, shared
        self.sent, self.arrived = buffers[0:2]
        self.modes_out, self.modes_in, self.mixed_out, self.mixed_in = buffers[2:6]
        self.planes_out = buffers[6]
        by_space = lambda ref: lambda peer, s: ref.at[peer, s]
        by_dp = lambda ref: lambda peer, s: ref.at[s, peer]
        self.to_modes = Exchange("space", SPACE, by_space(self.sent), by_space(self.arrived), sems[0:3])
        self.to_weights = Exchange("dp", DP, by_dp(self.modes_out), by_dp(self.modes_in), sems[3:6])
        self.from_weights = Exchange("dp", DP, by_dp(self.mixed_out), by_dp(self.mixed_in), sems[6:9])
        self.to_planes = Exchange("space", SPACE, by_space(self.planes_out), by_space(final), sems[9:12])

    def modes(self, s):
        to_modes, _, turn, _, rows, _, _ = self.shared
        self.to_modes.arrive(s)
        modes_of_sample(s, self.arrived, to_modes, turn, rows, self.modes_out)
        self.to_weights.start(s)

    def mix(self, s):
        _, _, _, wide, rows, mixed_rows, _ = self.shared
        self.to_weights.arrive(s)
        mix_sample(s, self.backward, self.modes_in, wide, rows, mixed_rows, self.mixed_out)
        self.from_weights.start(s)

    def planes(self, s):
        _, to_planes, _, _, rows, _, planes = self.shared
        self.from_weights.arrive(s)
        planes_of_sample(s, self.mixed_in, to_planes, rows, planes, self.planes_out)
        self.to_planes.start(s)

    def leave(self):
        for exchange in (self.to_modes, self.to_weights, self.from_weights, self.to_planes):
            for s in range(HERE):
                exchange.leave(s)


N_TABLES = 7


def layer_kernel(*refs):
    refs = list(refs)

    def take(count):
        taken = refs[:count]
        del refs[:count]
        return taken

    field_hbm, cotangent_hbm, point_ref, bias_ref = take(4)
    tables_hbm = take(N_TABLES)
    pre_grad_hbm, returned, weight_grad = take(3)
    field, cotangent = take(2)
    tables = take(N_TABLES)
    forward_buffers = take(8)
    backward_buffers = take(7)
    point, wide, rows, mixed_rows, planes, operand = take(6)
    field_sem, cotangent_sem, pre_grad_sem, table_sem = take(4)
    forward_sems, backward_sems = take(12), take(12)
    weight, grid, inverse, to_modes, to_planes, factors, turn = tables

    def load(s, pair, source, target, sems):
        return pltpu.make_async_copy(
            source.at[s, pl.ds(2 * pair, 2)], target.at[s, pl.ds(2 * pair, 2)], sems.at[s, pair]
        )

    def keep(s, pair):
        return load(s, pair, cotangent, pre_grad_hbm, pre_grad_sem)

    def each_pair(body):
        def step(pair, carry):
            body(pair)
            return carry

        lax.fori_loop(0, PAIRS, step, 0)

    def table_copy(i):
        return pltpu.make_async_copy(tables_hbm[i], tables[i], table_sem.at[i])

    barrier = greet()
    table_copy(1).start()
    table_copy(5).start()
    each_pair(lambda pair: load(0, pair, field_hbm, field, field_sem).start())
    for i in (0, 2, 3, 4, 6):
        table_copy(i).start()
    each_pair(lambda pair: load(1, pair, field_hbm, field, field_sem).start())
    for s in range(HERE):
        each_pair(lambda pair: load(s, pair, cotangent_hbm, cotangent, cotangent_sem).start())

    shared = (to_modes, to_planes, turn, wide, rows, mixed_rows, planes)
    ahead = Pass(False, forward_buffers[:7], forward_buffers[7], forward_sems, shared)
    back = Pass(True, backward_buffers, returned, backward_sems, shared)

    def forward(s):
        def body(pair):
            load(s, pair, field_hbm, field, field_sem).wait()
            here = (field[s, 2 * pair], field[s, 2 * pair + 1])
            forward_pair(grid, factors.at[0], here, planes, pair)

        each_pair(body)
        store_forward(planes, ahead.sent, s)

    def middle(s):
        bias = jnp.concatenate([bias_ref[...], bias_ref[...]], axis=1)

        def body(pair):
            load(s, pair, cotangent_hbm, cotangent, cotangent_sem).wait()
            inverse_operand(
                lambda w, plane, part: forward_buffers[7][w, s, 2 * pair + plane, part],
                factors.at[1],
                operand,
            )

            def cell(plane, h, value):
                lanes = slice(h * LANES, (h + 1) * LANES)
                upstream = cotangent[s, 2 * pair + plane, :, lanes].astype(F32)
                grad = upstream * gelu_slope(value + bias)
                cotangent[s, 2 * pair + plane, :, lanes] = grad.astype(BF16)

            here = (field[s, 2 * pair], field[s, 2 * pair + 1])
            on_cells(here, inverse, operand, point, False, cell)
            keep(s, pair).start()
            there = (cotangent[s, 2 * pair], cotangent[s, 2 * pair + 1])
            forward_pair(grid, factors.at[1], there, planes, pair)

        each_pair(body)
        store_forward(planes, back.sent, s)

    table_copy(1).wait()
    table_copy(5).wait()
    forward(0)
    pl.semaphore_wait(barrier, SPACE + DP - 2)
    ahead.to_modes.start(0)
    forward(1)
    ahead.to_modes.start(1)
    for i in (0, 2, 3, 4, 6):
        table_copy(i).wait()
    widen(weight, wide)
    spread_point(point_ref, point)
    for one in (ahead, back):
        if one is back:
            middle(0)
            back.to_modes.start(0)
            ahead.to_planes.arrive(1)
            middle(1)
            back.to_modes.start(1)
        one.modes(0)
        one.mix(0)
        one.modes(1)
        one.planes(0)
        one.mix(1)
        if one is back:
            weight_gradient(ahead.modes_in, back.modes_in, rows, mixed_rows, weight_grad)
        one.planes(1)
        one.to_planes.arrive(0)
    back.to_planes.arrive(1)
    ahead.leave()
    back.leave()
    for s in range(HERE):
        each_pair(lambda pair: keep(s, pair).wait())


def final_kernel(
    arrived_ref, pre_grad_ref, inverse_ref, factor_ref, point_ref, weight_grad_ref, out_ref, kept_ref, operand, point
):
    @pl.when((pl.program_id(0) == 0) & (pl.program_id(1) == 0))
    def _():
        spread_point(point_ref, point)

    kept_ref[...] = weight_grad_ref[...]
    inverse_operand(
        lambda w, plane, part: arrived_ref[w, 0, plane, part], factor_ref.at[0], operand
    )

    def body(plane, h, value):
        out_ref[0, plane, :, h * LANES : (h + 1) * LANES] = value.astype(BF16)

    on_cells((pre_grad_ref[0, 0], pre_grad_ref[0, 1]), inverse_ref, operand, point, True, body)


def whole(shape):
    return pl.BlockSpec(shape, lambda s, pair: (0,) * len(shape))


def params(mib):
    return pltpu.CompilerParams(vmem_limit_bytes=mib * 1024 * 1024)


GRID_BLOCK = pl.BlockSpec((1, 2, G, G * C), lambda s, pair: (s, pair, 0, 0))
ARRIVED_BLOCK = pl.BlockSpec((SPACE, 1, 2, 32, LANES), lambda s, pair: (0, s, pair, 0, 0))
SENT = jax.ShapeDtypeStruct((SPACE, HERE, K, 16, LANES), BF16)
MODES = jax.ShapeDtypeStruct((HERE, DP, 32, LANES), BF16)
RETURNED = jax.ShapeDtypeStruct((SPACE, HERE, PLANES, 32, LANES), BF16)
ROWS_SCRATCH = pltpu.VMEM((DP * 32, LANES), F32)
OPERAND_SCRATCH = pltpu.VMEM((2, K * K, 2 * LANES), BF16)
ANYWHERE = pl.BlockSpec(memory_space=pl.ANY)
IN_VMEM = pl.BlockSpec(memory_space=pltpu.VMEM)
SENT_SCRATCH = pltpu.VMEM((SPACE * 256, LANES), F32)


def on_device(field, cotangent, spectral_weight, point_weight, bias):
    table = grid_table()
    tables = [
        spectral_weight,
        jnp.asarray(bf16_table(table)),
        jnp.asarray(bf16_table(table.transpose(0, 2, 1))),
        jnp.asarray(bf16_table(plane_table())),
        jnp.asarray(bf16_table(plane_inverse_table())),
        jnp.asarray(np.stack([cell_factor(False), cell_factor(True)])),
        jnp.asarray(plane_factor()),
    ]
    weight_grad_type = jax.ShapeDtypeStruct(spectral_weight.shape, F32)
    grid_type = jax.ShapeDtypeStruct(field.shape, BF16)
    buffers = [pltpu.VMEM(SENT.shape, BF16)] * 2
    buffers += [pltpu.VMEM(MODES.shape, BF16)] * 4
    buffers += [pltpu.VMEM(RETURNED.shape, BF16)]
    sems = []
    for size in (SPACE, DP, DP, SPACE):
        sems += [
            pltpu.SemaphoreType.DMA((HERE, size)),
            pltpu.SemaphoreType.DMA((HERE, size)),
            pltpu.SemaphoreType.DMA((HERE,)),
        ]
    pre_grad, arrived, weight_grad = pl.pallas_call(
        layer_kernel,
        in_specs=[ANYWHERE, ANYWHERE, IN_VMEM, IN_VMEM] + [ANYWHERE] * N_TABLES,
        out_specs=[ANYWHERE, ANYWHERE, IN_VMEM],
        out_shape=[grid_type, RETURNED, weight_grad_type],
        scratch_shapes=[pltpu.VMEM(field.shape, BF16)] * 2
        + [pltpu.VMEM(table.shape, table.dtype) for table in tables]
        + buffers
        + [pltpu.VMEM(RETURNED.shape, BF16)]
        + buffers
        + [
            pltpu.VMEM((2 * LANES, 2 * LANES), BF16),
            pltpu.VMEM((32, LANES, LANES), BF16),
            ROWS_SCRATCH,
            ROWS_SCRATCH,
            SENT_SCRATCH,
            OPERAND_SCRATCH,
        ]
        + [pltpu.SemaphoreType.DMA((HERE, PAIRS))] * 3
        + [pltpu.SemaphoreType.DMA((N_TABLES,))]
        + sems
        + sems,
        compiler_params=pltpu.CompilerParams(
            vmem_limit_bytes=56 * 1024 * 1024, collective_id=0, has_side_effects=True
        ),
        name="layer",
    )(field, cotangent, point_weight, bias[None, :], *tables)
    weight_block = pl.BlockSpec((2, 2, C, LANES), lambda s, pair: (s * PAIRS + pair, 0, 0, 0))
    field_grad, weight_grad = pl.pallas_call(
        final_kernel,
        grid=(HERE, PAIRS),
        in_specs=[
            ARRIVED_BLOCK,
            GRID_BLOCK,
            whole(tables[2].shape),
            whole(tables[5].shape),
            whole(point_weight.shape),
            weight_block,
        ],
        out_specs=[GRID_BLOCK, weight_block],
        out_shape=[grid_type, weight_grad_type],
        scratch_shapes=[OPERAND_SCRATCH, pltpu.VMEM((2 * LANES, 2 * LANES), BF16)],
        compiler_params=params(56),
        name="final",
    )(arrived, pre_grad, tables[2], tables[5], point_weight, weight_grad)
    return (field_grad, weight_grad)


def solution(mesh):
    return jax.shard_map(
        on_device,
        mesh=mesh,
        in_specs=(
            P("dp", "space", None, None),
            P("dp", "space", None, None),
            P("dp", "space", None, None),
            P(),
            P(),
        ),
        out_specs=(P("dp", "space", None, None), P("dp", "space", None, None)),
        check_vma=False,
    )
```

```python
import jax
import jax.numpy as jnp
import ml_dtypes
import numpy as np
from jax import lax
from jax.experimental import pallas as pl
from jax.experimental.pallas import tpu as pltpu
from jax.sharding import PartitionSpec as P

C = 64
K = 16
G = 64
H = G // 2
LANES = 2 * C
PLANES = 8
PAIRS = PLANES // 2
SPACE = 8
DP = 16
HERE = 2
SAMPLES = 32
F32 = jnp.float32
BF16 = jnp.bfloat16


def cosine(turns):
    return np.cos(2.0 * np.pi * (turns % G) / G)


def sine(turns):
    return np.sin(2.0 * np.pi * (turns % G) / G)


def grid_table():
    freq = np.arange(K)
    signed = np.where(freq < K // 2, freq, freq - K)
    k3 = freq.reshape(K // 2, 2).T
    turns = (
        signed[None, :, None, None, None] * np.arange(G)
        + k3[:, None, :, None, None] * 2 * np.arange(H // 2)[:, None]
    )
    table = np.stack([cosine(turns), -sine(turns)], axis=2) / G
    return table.reshape(2, K * K, G * H // 2)


def plane_table():
    freq = np.arange(K)
    signed = np.where(freq < K // 2, freq, freq - K)
    planes = (PLANES * np.arange(SPACE)[:, None] + 2 * np.arange(PAIRS)[None, :]).reshape(SPACE, 2, 2)
    turns = signed[:, None, None, None] * planes[None]
    cos, sin = cosine(turns) / 8.0, sine(turns) / 8.0
    table = np.zeros((2, 2, 2, K, SPACE, 2, 2, 2, 2, 2))
    for b in range(2):
        for j in range(2):
            table[b, j, 0, :, :, :, b, j, 0] = cos
            table[b, j, 0, :, :, :, b, j, 1] = sin
            table[b, j, 1, :, :, :, b, j, 0] = -sin
            table[b, j, 1, :, :, :, b, j, 1] = cos
    return table.reshape(8 * K, SPACE * 32)


def plane_inverse_table():
    freq = np.arange(K)
    signed = np.where(freq < K // 2, freq, freq - K)
    turns = (PLANES * np.arange(SPACE)[:, None, None] + np.arange(PLANES)[None, :, None]) * signed
    cos, sin = cosine(turns) / 8.0, sine(turns) / 8.0
    table = np.zeros((SPACE, 2, PLANES, 2, K))
    table[:, 0, :, 0] = cos
    table[:, 0, :, 1] = -sin
    table[:, 1, :, 0] = sin
    table[:, 1, :, 1] = cos
    return table.reshape(SPACE * 2 * PLANES, 2 * K)


def cell_factor(weighted):
    freq = np.arange(K)
    weight = np.where(freq == 0, 1.0, 2.0) if weighted else np.ones(K)
    out = np.zeros((2, K, 2, C))
    out[0, :, 0] = weight[:, None]
    out[0, :, 1] = (weight * cosine(freq))[:, None]
    out[1, :, 1] = (weight * sine(freq))[:, None]
    out = out.reshape(2, K // 2, 2, LANES).transpose(2, 0, 1, 3)
    return np.ascontiguousarray(out, dtype=np.float32)


def plane_factor():
    freq = np.arange(K)
    signed = np.where(freq < K // 2, freq, freq - K)
    out = np.zeros((2, K, 2, C))
    out[0, :, 0] = 1.0
    out[0, :, 1] = cosine(signed)[:, None]
    out[1, :, 1] = sine(signed)[:, None]
    return out.reshape(2, K, LANES).astype(np.float32)


def bf16_table(values):
    return np.asarray(values, np.float32).astype(ml_dtypes.bfloat16)


def low_lanes(rows):
    return lax.broadcasted_iota(jnp.int32, (rows, LANES), 1) < C


def swap_halves(tile):
    return pltpu.roll(tile, C, 1)


def fold_halves(low, first, second):
    return jnp.where(low, first, second) + swap_halves(jnp.where(low, second, first))


def cell_tiles(planes, h):
    lanes = slice(h * LANES, (h + 1) * LANES)
    return jnp.concatenate([plane[:, lanes] for plane in planes], axis=1)


def forward_pair(table_ref, factor_ref, planes, scratch, pair):
    low = low_lanes(K // 2)
    for b in range(2):
        parts = []
        for h in range(H // 2):
            near, far = cell_tiles(planes, h), cell_tiles(planes, h + H // 2)
            parts.append(near - far if b else near + far)
        modes = jnp.dot(
            table_ref[b], jnp.concatenate(parts, axis=0), preferred_element_type=F32
        )
        cos, sin = factor_ref[b, 0], factor_ref[b, 1]
        for j2 in range(K):
            halves = ([], [])
            for plane in range(2):
                lanes = slice(plane * LANES, (plane + 1) * LANES)
                real = modes[j2 * K : j2 * K + 8, lanes]
                imag = modes[j2 * K + 8 : j2 * K + 16, lanes]
                halves[0].append(real * cos + imag * sin)
                halves[1].append(imag * cos - real * sin)
            for q in range(2):
                start = (j2 // 2) * 128 + b * 8 + (j2 % 2) * 4 + q * 2 + pair
                scratch[pl.ds(start, 8, stride=16), :] = fold_halves(low, *halves[q])


def store_forward(scratch, out, chunk):
    for p in range(SPACE):
        out[p, chunk] = scratch[p * 128 : (p + 1) * 128, :].reshape(8, 16, LANES).astype(BF16)


def modes_of_sample(s, arrived, table_ref, factor_ref, rows, out):
    low = low_lanes(K)
    cos, sin = factor_ref[0], factor_ref[1]
    operand = jnp.concatenate(
        [
            jnp.concatenate(
                [arrived[w, 2 * s + half, k] for w in range(SPACE) for half in range(2)], axis=0
            )
            for k in range(8)
        ],
        axis=1,
    )
    modes = jnp.dot(table_ref[...], operand, preferred_element_type=F32)
    for k in range(8):
        lanes = slice(k * LANES, (k + 1) * LANES)
        for b in range(2):
            for j in range(2):
                row = (b * 2 + j) * 32
                real = modes[row : row + K, lanes]
                imag = modes[row + K : row + 2 * K, lanes]
                rows[pl.ds((2 * k + b) * 2 + j, K, stride=32), :] = fold_halves(
                    low, real * cos + imag * sin, imag * cos - real * sin
                )
    out[s] = rows[...].reshape(DP, 32, LANES).astype(BF16)


def widen(weight_ref, wide):
    low = low_lanes(C)
    for item in range(32):
        top = weight_ref[item // 2, item % 2]
        turned = swap_halves(top.astype(F32))
        wide[item, :C] = top
        wide[item, C:] = jnp.where(low, -turned, turned).astype(BF16)


def mix_sample(s, backward, modes, wide, rows, mixed_rows, out):
    rows[...] = modes[s].reshape(DP * 32, LANES).astype(F32)
    dims = (((1,), (1,)), ((), ())) if backward else (((1,), (0,)), ((), ()))
    for item in range(32):
        here = pl.ds(item, DP, stride=32)
        mixed_rows[here, :] = lax.dot_general(
            rows[here, :].astype(BF16), wide[item], dims, preferred_element_type=F32
        )
    out[s] = mixed_rows[...].reshape(DP, 32, LANES).astype(BF16)


def weight_gradient(field_modes, grad_modes, rows, mixed_rows, weight_grad_ref):
    low = low_lanes(C)
    for s in range(HERE):
        rows[...] = field_modes[s].reshape(DP * 32, LANES).astype(F32)
        mixed_rows[...] = grad_modes[s].reshape(DP * 32, LANES).astype(F32)
        for item in range(32):
            here = pl.ds(item, DP, stride=32)
            outer = lax.dot_general(
                rows[here, :].astype(BF16),
                mixed_rows[here, :].astype(BF16),
                (((0,), (0,)), ((), ())),
                preferred_element_type=F32,
            )
            turned = swap_halves(outer[C:])
            term = (outer[:C] + jnp.where(low, turned, -turned)) * (1.0 / SAMPLES)
            if s == 0:
                weight_grad_ref[item // 2, item % 2] = term
            else:
                weight_grad_ref[item // 2, item % 2] += term


def planes_of_sample(s, mixed, table_ref, rows, planes, out):
    low = low_lanes(K)
    rows[...] = mixed[s].reshape(DP * 32, LANES).astype(F32)
    columns = []
    for k3 in range(K):
        first = rows[pl.ds(k3 * 2, K, stride=32), :]
        second = rows[pl.ds(k3 * 2 + 1, K, stride=32), :]
        real = jnp.where(low, first, swap_halves(second))
        imag = jnp.where(low, swap_halves(first), second)
        columns.append(jnp.concatenate([real, imag], axis=0).astype(BF16))
    partial = jnp.dot(
        table_ref[...], jnp.concatenate(columns, axis=1), preferred_element_type=F32
    )
    for p in range(SPACE):
        for r in range(2):
            row = (p * 2 + r) * PLANES
            for k3 in range(K):
                start = p * 256 + (k3 % 2) * 16 + r * 8 + k3 // 2
                planes[pl.ds(start, PLANES, stride=32), :] = partial[
                    row : row + PLANES, k3 * LANES : (k3 + 1) * LANES
                ]
        for half in range(2):
            start = p * 256 + half * 128
            out[p, 2 * s + half] = planes[start : start + 128, :].reshape(4, 32, LANES).astype(BF16)


class Exchange:
    def __init__(self, axis, size, source, target, sems, far=()):
        self.axis, self.size, self.source, self.target = axis, size, source, target
        self.send, self.recv, self.own = sems
        self.me = lax.axis_index(axis)
        self.far = far
        self.away = []

    def remote(self, s, slot, peer):
        return pltpu.make_async_remote_copy(
            src_ref=self.source(peer, s),
            dst_ref=self.target(slot, s),
            send_sem=self.send.at[s, peer],
            recv_sem=self.recv.at[s, slot],
            device_id={self.axis: peer},
            device_id_type=pl.DeviceIdType.MESH,
        )

    def local(self, s):
        return pltpu.make_async_copy(
            self.source(self.me, s), self.target(self.me, s), self.own.at[s]
        )

    def peers(self, body):
        def step(offset, carry):
            body(lax.rem(self.me + offset, self.size))
            return carry

        lax.fori_loop(1, self.size, step, 0)

    def start(self, s, after=None):
        def one(peer):
            if after is not None:
                self.remote(after, self.me, peer).wait_send()
            self.remote(s, self.me, peer).start()

        self.peers(one)
        if s in self.far:
            self.local(s).start()
        else:
            self.target(self.me, s)[...] = self.source(self.me, s)[...]
        if after is not None:
            self.away.remove(after)
        self.away.append(s)

    def arrive(self, s):
        self.peers(lambda peer: self.remote(s, peer, peer).wait_recv())
        if s in self.far:
            self.local(s).wait()

    def leave(self):
        for s in self.away:
            self.peers(lambda peer: self.remote(s, self.me, peer).wait_send())


def greet():
    barrier = pltpu.get_barrier_semaphore()
    for axis, size in (("space", SPACE), ("dp", DP)):
        me = lax.axis_index(axis)

        def step(offset, carry):
            pl.semaphore_signal(
                barrier,
                inc=1,
                device_id={axis: lax.rem(me + offset, size)},
                device_id_type=pl.DeviceIdType.MESH,
            )
            return carry

        lax.fori_loop(1, size, step, 0)
    return barrier


def inverse_operand(tile_of, factor_ref, operand_ref):
    low = low_lanes(8)
    for plane in range(2):
        for b in range(2):
            cos, sin = factor_ref[b, 0], factor_ref[b, 1]
            for w in range(SPACE):
                tile = tile_of(w, plane, slice(b * 16, (b + 1) * 16)).astype(F32)
                real, imag = tile[:8], tile[8:]
                real_turned, imag_turned = swap_halves(real), swap_halves(imag)
                for j in range(2):
                    if j == 0:
                        re = jnp.where(low, real, real_turned)
                        im = jnp.where(low, imag, imag_turned)
                    else:
                        re = jnp.where(low, real_turned, real)
                        im = jnp.where(low, imag_turned, imag)
                    waves = jnp.concatenate([re * cos - im * sin, im * cos + re * sin], axis=0)
                    row = (2 * w + j) * 16
                    operand_ref[b, row : row + 16, plane * LANES : (plane + 1) * LANES] = waves.astype(BF16)


def on_cells(planes, inverse_ref, operand_ref, point_ref, back, body):
    depth = 4
    dims = (((1,), (1 if back else 0,)), ((), ()))
    for block in range(H // 2 // depth):
        rows = slice(block * depth * G, (block + 1) * depth * G)
        even = jnp.dot(inverse_ref[0, rows], operand_ref[0], preferred_element_type=F32)
        odd = jnp.dot(inverse_ref[1, rows], operand_ref[1], preferred_element_type=F32)
        for side in range(2):
            first = block * depth + side * (H // 2)
            cells = jnp.concatenate([cell_tiles(planes, first + i) for i in range(depth)], axis=0)
            local = lax.dot_general(cells, point_ref[...], dims, preferred_element_type=F32)
            total = local + (even - odd if side else even + odd)
            for i in range(depth):
                for plane in range(2):
                    body(
                        plane,
                        first + i,
                        total[i * G : (i + 1) * G, plane * LANES : (plane + 1) * LANES],
                    )


def gelu_slope(values):
    normal_cdf = 0.5 * (1.0 + lax.erf(values * 0.7071067811865476))
    density = jnp.exp(-0.5 * values * values) * 0.3989422804014327
    return normal_cdf + values * density


def spread_point(point_ref, point):
    low = low_lanes(C)
    twice = jnp.concatenate([point_ref[...], point_ref[...]], axis=1).astype(F32)
    none = jnp.zeros((LANES, LANES), BF16)
    both = jnp.concatenate(
        [jnp.where(low, twice, 0.0), jnp.where(low, 0.0, twice)], axis=0
    ).astype(BF16)
    point[:LANES, :LANES] = both
    point[:LANES, LANES:] = none
    point[LANES:, :LANES] = none
    point[LANES:, LANES:] = both


class Pass:
    def __init__(self, backward, buffers, final, sems, shared):
        self.backward, self.shared = backward, shared
        self.sent, self.arrived = buffers[0:2]
        self.modes_out, self.modes_in, self.mixed_out, self.mixed_in = buffers[2:6]
        self.planes_out = buffers[6]
        by_space = lambda ref: lambda peer, s: ref.at[peer, s]
        by_dp = lambda ref: lambda peer, s: ref.at[s, peer]
        self.to_modes = Exchange("space", SPACE, by_space(self.sent), by_space(self.arrived), sems[0:3])
        self.to_weights = Exchange("dp", DP, by_dp(self.modes_out), by_dp(self.modes_in), sems[3:6])
        self.from_weights = Exchange("dp", DP, by_dp(self.mixed_out), by_dp(self.mixed_in), sems[6:9])
        self.to_planes = Exchange("space", SPACE, by_space(self.planes_out), final, sems[9:12], (2, 3) if backward else ())

    def modes(self, s):
        to_modes, _, turn, _, rows, _, _ = self.shared
        self.to_modes.arrive(2 * s)
        self.to_modes.arrive(2 * s + 1)
        modes_of_sample(s, self.arrived, to_modes, turn, rows, self.modes_out)
        self.to_weights.start(s)

    def mix(self, s):
        _, _, _, wide, rows, mixed_rows, _ = self.shared
        self.to_weights.arrive(s)
        mix_sample(s, self.backward, self.modes_in, wide, rows, mixed_rows, self.mixed_out)
        self.from_weights.start(s)

    def planes(self, s):
        _, to_planes, _, _, rows, _, planes = self.shared
        self.from_weights.arrive(s)
        planes_of_sample(s, self.mixed_in, to_planes, rows, planes, self.planes_out)

    def leave(self):
        for exchange in (self.to_modes, self.to_weights, self.from_weights, self.to_planes):
            exchange.leave()


N_TABLES = 7


def layer_kernel(*refs):
    refs = list(refs)

    def take(count):
        taken = refs[:count]
        del refs[:count]
        return taken

    field_hbm, cotangent_hbm, point_ref, bias_ref = take(4)
    tables_hbm = take(N_TABLES)
    pre_grad_hbm, done_hbm, returned, weight_grad = take(4)
    field, cotangent = take(2)
    tables = take(N_TABLES)
    forward_buffers = take(8)
    backward_buffers = take(8)
    point, wide, rows, mixed_rows, planes, operand = take(6)
    came, came_back = forward_buffers[7], backward_buffers[7]
    field_sem, cotangent_sem, out_sem, table_sem = take(4)
    forward_sems, backward_sems = take(12), take(12)
    weight, grid, inverse, to_modes, to_planes, factors, turn = tables

    def load(s, pair, source, target, sems):
        return pltpu.make_async_copy(
            source.at[s, pl.ds(2 * pair, 2)], target.at[s, pl.ds(2 * pair, 2)], sems.at[s, pair]
        )

    def keep(s, pair):
        source, target = (cotangent, pre_grad_hbm) if s else (field, done_hbm)
        return pltpu.make_async_copy(
            source.at[s, pl.ds(2 * pair, 2)], target.at[pl.ds(2 * pair, 2)], out_sem.at[s, pair]
        )

    def each_pair(body):
        def step(pair, carry):
            body(pair)
            return carry

        lax.fori_loop(0, PAIRS, step, 0)

    def table_copy(i):
        return pltpu.make_async_copy(tables_hbm[i], tables[i], table_sem.at[i])

    barrier = greet()
    table_copy(1).start()
    table_copy(5).start()
    each_pair(lambda pair: load(0, pair, field_hbm, field, field_sem).start())
    shared = (to_modes, to_planes, turn, wide, rows, mixed_rows, planes)
    ahead = Pass(
        False, forward_buffers[:7], lambda peer, c: came.at[peer, c], forward_sems, shared
    )
    back = Pass(
        True,
        backward_buffers[:7],
        lambda peer, c: returned.at[peer, c - 2] if c >= 2 else came_back.at[peer, c],
        backward_sems,
        shared,
    )

    def each_of_half(body):
        def step(inner, carry):
            body(inner)
            return carry

        lax.fori_loop(0, 2, step, 0)

    def forward(s, half):
        def body(inner):
            pair = 2 * half + inner
            load(s, pair, field_hbm, field, field_sem).wait()
            here = (field[s, 2 * pair], field[s, 2 * pair + 1])
            forward_pair(grid, factors.at[0], here, planes, inner)

        each_of_half(body)
        store_forward(planes, ahead.sent, 2 * s + half)

    def middle(s, half):
        bias = jnp.concatenate([bias_ref[...], bias_ref[...]], axis=1)
        ahead.to_planes.arrive(2 * s + half)

        def body(inner):
            pair = 2 * half + inner
            load(s, pair, cotangent_hbm, cotangent, cotangent_sem).wait()
            inverse_operand(
                lambda w, plane, part: came[w, 2 * s + half, 2 * inner + plane, part],
                factors.at[1],
                operand,
            )

            def cell(plane, h, value):
                lanes = slice(h * LANES, (h + 1) * LANES)
                upstream = cotangent[s, 2 * pair + plane, :, lanes].astype(F32)
                grad = upstream * gelu_slope(value + bias)
                cotangent[s, 2 * pair + plane, :, lanes] = grad.astype(BF16)

            here = (field[s, 2 * pair], field[s, 2 * pair + 1])
            on_cells(here, inverse, operand, point, False, cell)
            if s:
                keep(s, pair).start()
            there = (cotangent[s, 2 * pair], cotangent[s, 2 * pair + 1])
            forward_pair(grid, factors.at[1], there, planes, inner)

        each_of_half(body)
        store_forward(planes, back.sent, 2 * s + half)

    def last(half):
        back.to_planes.arrive(half)

        def body(inner):
            pair = 2 * half + inner
            inverse_operand(
                lambda w, plane, part: came_back[w, half, 2 * inner + plane, part], factors.at[0], operand
            )

            def cell(plane, h, value):
                field[0, 2 * pair + plane, :, h * LANES : (h + 1) * LANES] = value.astype(BF16)

            here = (cotangent[0, 2 * pair], cotangent[0, 2 * pair + 1])
            on_cells(here, inverse, operand, point, True, cell)
            keep(0, pair).start()

        each_of_half(body)

    table_copy(1).wait()
    table_copy(5).wait()
    forward(0, 0)
    pl.semaphore_wait(barrier, SPACE + DP - 2)
    ahead.to_modes.start(0)
    each_pair(lambda pair: load(1, pair, field_hbm, field, field_sem).start())
    for i in (0, 2, 3, 4, 6):
        table_copy(i).start()
    forward(0, 1)
    ahead.to_modes.start(1)
    forward(1, 0)
    for i in (0, 2, 3, 4, 6):
        table_copy(i).wait()
    ahead.to_modes.start(2, after=0)
    for s in range(HERE):
        each_pair(lambda pair: load(s, pair, cotangent_hbm, cotangent, cotangent_sem).start())
    forward(1, 1)
    widen(weight, wide)
    spread_point(point_ref, point)
    ahead.to_modes.start(3, after=1)
    ahead.modes(0)
    ahead.mix(0)
    ahead.modes(1)
    ahead.planes(0)
    ahead.to_planes.start(0)
    ahead.mix(1)
    ahead.to_planes.start(1, after=0)
    ahead.planes(1)
    ahead.to_planes.start(2)
    ahead.to_planes.start(3)
    middle(0, 0)
    back.to_modes.start(0)
    middle(0, 1)
    back.to_modes.start(1)
    middle(1, 0)
    back.to_modes.start(2)
    back.modes(0)
    middle(1, 1)
    back.to_modes.start(3)
    back.mix(0)
    back.modes(1)
    back.planes(0)
    back.to_planes.start(0)
    back.to_planes.start(1)
    back.mix(1)
    weight_gradient(ahead.modes_in, back.modes_in, rows, mixed_rows, weight_grad)
    back.planes(1)
    back.to_planes.start(2)
    back.to_planes.start(3)
    last(0)
    last(1)
    back.to_planes.arrive(2)
    back.to_planes.arrive(3)
    ahead.leave()
    back.leave()
    for s in range(HERE):
        each_pair(lambda pair: keep(s, pair).wait())


def final_kernel(
    returned,
    pre_grad_hbm,
    done_hbm,
    weight_grad_hbm,
    inverse,
    factors,
    point_ref,
    out_hbm,
    kept_hbm,
    came,
    pre_grad,
    out,
    done,
    weight_grad,
    operand,
    point,
    came_sem,
    pre_grad_sem,
    out_sem,
    done_sem,
    copy_sem,
):
    def came_copy(half):
        return pltpu.make_async_copy(returned.at[:, half], came.at[half], came_sem.at[half])

    def two(pair):
        return pl.ds(2 * pair, 2)

    def load(pair):
        return pltpu.make_async_copy(
            pre_grad_hbm.at[two(pair)], pre_grad.at[two(pair)], pre_grad_sem.at[pair]
        )

    def keep(pair):
        return pltpu.make_async_copy(out.at[two(pair)], out_hbm.at[1, two(pair)], out_sem.at[pair])

    def fetch(pair):
        return pltpu.make_async_copy(done_hbm.at[two(pair)], done.at[two(pair)], done_sem.at[pair])

    def pass_on(pair):
        return pltpu.make_async_copy(done.at[two(pair)], out_hbm.at[0, two(pair)], done_sem.at[pair])

    weight_in = pltpu.make_async_copy(weight_grad_hbm, weight_grad, copy_sem.at[0])
    weight_out = pltpu.make_async_copy(weight_grad, kept_hbm, copy_sem.at[1])
    for half in range(2):
        came_copy(half).start()
        load(2 * half).start()
        load(2 * half + 1).start()
    weight_in.start()
    for pair in range(PAIRS):
        fetch(pair).start()
    spread_point(point_ref, point)
    for half in range(2):
        came_copy(half).wait()

        def step(inner, carry):
            pair = 2 * half + inner
            load(pair).wait()
            inverse_operand(
                lambda w, plane, part: came[half, w, 2 * inner + plane, part], factors.at[0], operand
            )

            def cell(plane, h, value):
                out[2 * pair + plane, :, h * LANES : (h + 1) * LANES] = value.astype(BF16)

            here = (pre_grad[2 * pair], pre_grad[2 * pair + 1])
            on_cells(here, inverse, operand, point, True, cell)
            keep(pair).start()
            fetch(pair).wait()
            pass_on(pair).start()
            return carry

        lax.fori_loop(0, 2, step, 0)
        if half == 0:
            weight_in.wait()
            weight_out.start()
    for pair in range(PAIRS):
        keep(pair).wait()
        pass_on(pair).wait()
    weight_out.wait()


SENT = jax.ShapeDtypeStruct((SPACE, 2 * HERE, 8, 16, LANES), BF16)
MODES = jax.ShapeDtypeStruct((HERE, DP, 32, LANES), BF16)
RETURNED = jax.ShapeDtypeStruct((SPACE, 2 * HERE, 4, 32, LANES), BF16)
ONE_RETURNED = jax.ShapeDtypeStruct((SPACE, 2, 4, 32, LANES), BF16)
ROWS_SCRATCH = pltpu.VMEM((DP * 32, LANES), F32)
OPERAND_SCRATCH = pltpu.VMEM((2, K * K, 2 * LANES), BF16)
ANYWHERE = pl.BlockSpec(memory_space=pl.ANY)
IN_VMEM = pl.BlockSpec(memory_space=pltpu.VMEM)
SENT_SCRATCH = pltpu.VMEM((SPACE * 256, LANES), F32)


def on_device(field, cotangent, spectral_weight, point_weight, bias):
    table = grid_table()
    tables = [
        spectral_weight,
        jnp.asarray(bf16_table(table)),
        jnp.asarray(bf16_table(table.transpose(0, 2, 1))),
        jnp.asarray(bf16_table(plane_table())),
        jnp.asarray(bf16_table(plane_inverse_table())),
        jnp.asarray(np.stack([cell_factor(False), cell_factor(True)])),
        jnp.asarray(plane_factor()),
    ]
    weight_grad_type = jax.ShapeDtypeStruct(spectral_weight.shape, F32)
    grid_type = jax.ShapeDtypeStruct(field.shape, BF16)
    buffers = [pltpu.VMEM(SENT.shape, BF16)] * 2
    buffers += [pltpu.VMEM(MODES.shape, BF16)] * 4
    buffers += [pltpu.VMEM(RETURNED.shape, BF16)]
    sems = []
    for chunks, size in ((2 * HERE, SPACE), (HERE, DP), (HERE, DP), (2 * HERE, SPACE)):
        sems += [
            pltpu.SemaphoreType.DMA((chunks, size)),
            pltpu.SemaphoreType.DMA((chunks, size)),
            pltpu.SemaphoreType.DMA((chunks,)),
        ]
    sample_type = jax.ShapeDtypeStruct(field.shape[1:], BF16)
    pre_grad, done, arrived, weight_grad = pl.pallas_call(
        layer_kernel,
        in_specs=[ANYWHERE, ANYWHERE, IN_VMEM, IN_VMEM] + [ANYWHERE] * N_TABLES,
        out_specs=[ANYWHERE, ANYWHERE, ANYWHERE, IN_VMEM],
        out_shape=[sample_type, sample_type, ONE_RETURNED, weight_grad_type],
        scratch_shapes=[pltpu.VMEM(field.shape, BF16)] * 2
        + [pltpu.VMEM(table.shape, table.dtype) for table in tables]
        + buffers
        + [pltpu.VMEM(RETURNED.shape, BF16)]
        + buffers
        + [pltpu.VMEM(ONE_RETURNED.shape, BF16)]
        + [
            pltpu.VMEM((2 * LANES, 2 * LANES), BF16),
            pltpu.VMEM((32, LANES, LANES), BF16),
            ROWS_SCRATCH,
            ROWS_SCRATCH,
            SENT_SCRATCH,
            OPERAND_SCRATCH,
        ]
        + [pltpu.SemaphoreType.DMA((HERE, PAIRS))] * 3
        + [pltpu.SemaphoreType.DMA((N_TABLES,))]
        + sems
        + sems,
        compiler_params=pltpu.CompilerParams(
            vmem_limit_bytes=56 * 1024 * 1024, collective_id=0, has_side_effects=True
        ),
        name="layer",
    )(field, cotangent, point_weight, bias[None, :], *tables)
    field_grad, weight_grad = pl.pallas_call(
        final_kernel,
        in_specs=[ANYWHERE] * 4 + [IN_VMEM] * 3,
        out_specs=[ANYWHERE, ANYWHERE],
        out_shape=[grid_type, weight_grad_type],
        scratch_shapes=[
            pltpu.VMEM((2, SPACE, 4, 32, LANES), BF16),
            pltpu.VMEM(sample_type.shape, BF16),
            pltpu.VMEM(sample_type.shape, BF16),
            pltpu.VMEM(sample_type.shape, BF16),
            pltpu.VMEM(spectral_weight.shape, F32),
            OPERAND_SCRATCH,
            pltpu.VMEM((2 * LANES, 2 * LANES), BF16),
            pltpu.SemaphoreType.DMA((2,)),
            pltpu.SemaphoreType.DMA((PAIRS,)),
            pltpu.SemaphoreType.DMA((PAIRS,)),
            pltpu.SemaphoreType.DMA((PAIRS,)),
            pltpu.SemaphoreType.DMA((2,)),
        ],
        compiler_params=pltpu.CompilerParams(vmem_limit_bytes=60 * 1024 * 1024),
        name="final",
    )(arrived, pre_grad, done, weight_grad, tables[2], tables[5], point_weight)
    return (field_grad, weight_grad)


def solution(mesh):
    return jax.shard_map(
        on_device,
        mesh=mesh,
        in_specs=(
            P("dp", "space", None, None),
            P("dp", "space", None, None),
            P("dp", "space", None, None),
            P(),
            P(),
        ),
        out_specs=(P("dp", "space", None, None), P("dp", "space", None, None)),
        check_vma=False,
    )
```

```python
import jax
import jax.numpy as jnp
import ml_dtypes
import numpy as np
from jax import lax
from jax.experimental import pallas as pl
from jax.experimental.pallas import tpu as pltpu
from jax.sharding import PartitionSpec as P

C = 64
K = 16
G = 64
H = G // 2
LANES = 2 * C
PLANES = 8
PAIRS = PLANES // 2
SPACE = 8
DP = 16
HERE = 2
SAMPLES = 32
F32 = jnp.float32
BF16 = jnp.bfloat16


def cosine(turns):
    return np.cos(2.0 * np.pi * (turns % G) / G)


def sine(turns):
    return np.sin(2.0 * np.pi * (turns % G) / G)


def grid_table():
    freq = np.arange(K)
    signed = np.where(freq < K // 2, freq, freq - K)
    k3 = freq.reshape(K // 2, 2).T
    turns = (
        signed[None, :, None, None, None] * np.arange(G)
        + k3[:, None, :, None, None] * 2 * np.arange(H // 2)[:, None]
    )
    table = np.stack([cosine(turns), -sine(turns)], axis=2) / G
    return table.reshape(2, K * K, G * H // 2)


def plane_table():
    freq = np.arange(K)
    signed = np.where(freq < K // 2, freq, freq - K)
    planes = (PLANES * np.arange(SPACE)[:, None] + 2 * np.arange(PAIRS)[None, :]).reshape(SPACE, 2, 2)
    turns = signed[:, None, None, None] * planes[None]
    cos, sin = cosine(turns) / 8.0, sine(turns) / 8.0
    table = np.zeros((2, 2, 2, K, SPACE, 2, 2, 2, 2, 2))
    for b in range(2):
        for j in range(2):
            table[b, j, 0, :, :, :, b, j, 0] = cos
            table[b, j, 0, :, :, :, b, j, 1] = sin
            table[b, j, 1, :, :, :, b, j, 0] = -sin
            table[b, j, 1, :, :, :, b, j, 1] = cos
    return table.reshape(8 * K, SPACE * 32)


def plane_inverse_table():
    freq = np.arange(K)
    signed = np.where(freq < K // 2, freq, freq - K)
    turns = (PLANES * np.arange(SPACE)[:, None, None] + np.arange(PLANES)[None, :, None]) * signed
    cos, sin = cosine(turns) / 8.0, sine(turns) / 8.0
    table = np.zeros((SPACE, 2, PLANES, 2, K))
    table[:, 0, :, 0] = cos
    table[:, 0, :, 1] = -sin
    table[:, 1, :, 0] = sin
    table[:, 1, :, 1] = cos
    return table.reshape(SPACE * 2 * PLANES, 2 * K)


def cell_factor(weighted):
    freq = np.arange(K)
    weight = np.where(freq == 0, 1.0, 2.0) if weighted else np.ones(K)
    out = np.zeros((2, K, 2, C))
    out[0, :, 0] = weight[:, None]
    out[0, :, 1] = (weight * cosine(freq))[:, None]
    out[1, :, 1] = (weight * sine(freq))[:, None]
    out = out.reshape(2, K // 2, 2, LANES).transpose(2, 0, 1, 3)
    return np.ascontiguousarray(out, dtype=np.float32)


def plane_factor():
    freq = np.arange(K)
    signed = np.where(freq < K // 2, freq, freq - K)
    out = np.zeros((2, K, 2, C))
    out[0, :, 0] = 1.0
    out[0, :, 1] = cosine(signed)[:, None]
    out[1, :, 1] = sine(signed)[:, None]
    return out.reshape(2, K, LANES).astype(np.float32)


def bf16_table(values):
    return np.asarray(values, np.float32).astype(ml_dtypes.bfloat16)


def low_lanes(rows):
    return lax.broadcasted_iota(jnp.int32, (rows, LANES), 1) < C


def swap_halves(tile):
    return pltpu.roll(tile, C, 1)


def fold_halves(low, first, second):
    return jnp.where(low, first, second) + swap_halves(jnp.where(low, second, first))


def cell_tiles(planes, h):
    lanes = slice(h * LANES, (h + 1) * LANES)
    return jnp.concatenate([plane[:, lanes] for plane in planes], axis=1)


def forward_pair(table_ref, factor_ref, planes, scratch, pair):
    low = low_lanes(K // 2)
    for b in range(2):
        parts = []
        for h in range(H // 2):
            near, far = cell_tiles(planes, h), cell_tiles(planes, h + H // 2)
            parts.append(near - far if b else near + far)
        modes = jnp.dot(
            table_ref[b], jnp.concatenate(parts, axis=0), preferred_element_type=F32
        )
        cos, sin = factor_ref[b, 0], factor_ref[b, 1]
        for j2 in range(K):
            halves = ([], [])
            for plane in range(2):
                lanes = slice(plane * LANES, (plane + 1) * LANES)
                real = modes[j2 * K : j2 * K + 8, lanes]
                imag = modes[j2 * K + 8 : j2 * K + 16, lanes]
                halves[0].append(real * cos + imag * sin)
                halves[1].append(imag * cos - real * sin)
            for q in range(2):
                start = (j2 // 2) * 128 + b * 8 + (j2 % 2) * 4 + q * 2 + pair
                scratch[pl.ds(start, 8, stride=16), :] = fold_halves(low, *halves[q])


def store_forward(scratch, out, chunk):
    for p in range(SPACE):
        out[p, chunk] = scratch[p * 128 : (p + 1) * 128, :].reshape(8, 16, LANES).astype(BF16)


def modes_of_sample(s, arrived, table_ref, factor_ref, rows, out):
    low = low_lanes(K)
    cos, sin = factor_ref[0], factor_ref[1]
    operand = jnp.concatenate(
        [
            jnp.concatenate(
                [arrived[w, 2 * s + half, k] for w in range(SPACE) for half in range(2)], axis=0
            )
            for k in range(8)
        ],
        axis=1,
    )
    modes = jnp.dot(table_ref[...], operand, preferred_element_type=F32)
    for k in range(8):
        lanes = slice(k * LANES, (k + 1) * LANES)
        for b in range(2):
            for j in range(2):
                row = (b * 2 + j) * 32
                real = modes[row : row + K, lanes]
                imag = modes[row + K : row + 2 * K, lanes]
                rows[pl.ds((2 * k + b) * 2 + j, K, stride=32), :] = fold_halves(
                    low, real * cos + imag * sin, imag * cos - real * sin
                )
    out[s] = rows[...].reshape(DP, 32, LANES).astype(BF16)


def widen(weight_ref, wide):
    low = low_lanes(C)
    for item in range(32):
        top = weight_ref[item // 2, item % 2]
        turned = swap_halves(top.astype(F32))
        wide[item, :C] = top
        wide[item, C:] = jnp.where(low, -turned, turned).astype(BF16)


def mix_sample(s, backward, modes, wide, rows, mixed_rows, out):
    rows[...] = modes[s].reshape(DP * 32, LANES).astype(F32)
    dims = (((1,), (1,)), ((), ())) if backward else (((1,), (0,)), ((), ()))
    for item in range(32):
        here = pl.ds(item, DP, stride=32)
        mixed_rows[here, :] = lax.dot_general(
            rows[here, :].astype(BF16), wide[item], dims, preferred_element_type=F32
        )
    out[s] = mixed_rows[...].reshape(DP, 32, LANES).astype(BF16)


def weight_gradient(field_modes, grad_modes, rows, mixed_rows, weight_grad_ref):
    low = low_lanes(C)
    for s in range(HERE):
        rows[...] = field_modes[s].reshape(DP * 32, LANES).astype(F32)
        mixed_rows[...] = grad_modes[s].reshape(DP * 32, LANES).astype(F32)
        for item in range(32):
            here = pl.ds(item, DP, stride=32)
            outer = lax.dot_general(
                rows[here, :].astype(BF16),
                mixed_rows[here, :].astype(BF16),
                (((0,), (0,)), ((), ())),
                preferred_element_type=F32,
            )
            turned = swap_halves(outer[C:])
            term = (outer[:C] + jnp.where(low, turned, -turned)) * (1.0 / SAMPLES)
            if s == 0:
                weight_grad_ref[item // 2, item % 2] = term
            else:
                weight_grad_ref[item // 2, item % 2] += term


def planes_of_sample(s, mixed, table_ref, rows, planes, out):
    low = low_lanes(K)
    rows[...] = mixed[s].reshape(DP * 32, LANES).astype(F32)
    columns = []
    for k3 in range(K):
        first = rows[pl.ds(k3 * 2, K, stride=32), :]
        second = rows[pl.ds(k3 * 2 + 1, K, stride=32), :]
        real = jnp.where(low, first, swap_halves(second))
        imag = jnp.where(low, swap_halves(first), second)
        columns.append(jnp.concatenate([real, imag], axis=0).astype(BF16))
    partial = jnp.dot(
        table_ref[...], jnp.concatenate(columns, axis=1), preferred_element_type=F32
    )
    for p in range(SPACE):
        for r in range(2):
            row = (p * 2 + r) * PLANES
            for k3 in range(K):
                start = p * 256 + (k3 % 2) * 16 + r * 8 + k3 // 2
                planes[pl.ds(start, PLANES, stride=32), :] = partial[
                    row : row + PLANES, k3 * LANES : (k3 + 1) * LANES
                ]
        for half in range(2):
            start = p * 256 + half * 128
            out[p, 2 * s + half] = planes[start : start + 128, :].reshape(4, 32, LANES).astype(BF16)


class Exchange:
    def __init__(self, axis, size, source, target, sems, far=()):
        self.axis, self.size, self.source, self.target = axis, size, source, target
        self.send, self.recv, self.own = sems
        self.me = lax.axis_index(axis)
        self.far = far
        self.away = []

    def remote(self, s, slot, peer):
        return pltpu.make_async_remote_copy(
            src_ref=self.source(peer, s),
            dst_ref=self.target(slot, s),
            send_sem=self.send.at[s, peer],
            recv_sem=self.recv.at[s, slot],
            device_id={self.axis: peer},
            device_id_type=pl.DeviceIdType.MESH,
        )

    def local(self, s):
        return pltpu.make_async_copy(
            self.source(self.me, s), self.target(self.me, s), self.own.at[s]
        )

    def peers(self, body):
        def step(offset, carry):
            body(lax.rem(self.me + offset, self.size))
            return carry

        lax.fori_loop(1, self.size, step, 0)

    def start(self, s, after=None):
        def one(peer):
            if after is not None:
                self.remote(after, self.me, peer).wait_send()
            self.remote(s, self.me, peer).start()

        self.peers(one)
        if s in self.far:
            self.local(s).start()
        else:
            self.target(self.me, s)[...] = self.source(self.me, s)[...]
        if after is not None:
            self.away.remove(after)
        self.away.append(s)

    def arrive(self, s):
        self.peers(lambda peer: self.remote(s, peer, peer).wait_recv())
        if s in self.far:
            self.local(s).wait()

    def leave(self):
        for s in self.away:
            self.peers(lambda peer: self.remote(s, self.me, peer).wait_send())


def greet():
    barrier = pltpu.get_barrier_semaphore()
    for axis, size in (("space", SPACE), ("dp", DP)):
        me = lax.axis_index(axis)

        def step(offset, carry):
            pl.semaphore_signal(
                barrier,
                inc=1,
                device_id={axis: lax.rem(me + offset, size)},
                device_id_type=pl.DeviceIdType.MESH,
            )
            return carry

        lax.fori_loop(1, size, step, 0)
    return barrier


def inverse_operand(tile_of, factor_ref, operand_ref):
    low = low_lanes(8)
    for plane in range(2):
        for b in range(2):
            cos, sin = factor_ref[b, 0], factor_ref[b, 1]
            for w in range(SPACE):
                tile = tile_of(w, plane, slice(b * 16, (b + 1) * 16)).astype(F32)
                real, imag = tile[:8], tile[8:]
                real_turned, imag_turned = swap_halves(real), swap_halves(imag)
                for j in range(2):
                    if j == 0:
                        re = jnp.where(low, real, real_turned)
                        im = jnp.where(low, imag, imag_turned)
                    else:
                        re = jnp.where(low, real_turned, real)
                        im = jnp.where(low, imag_turned, imag)
                    waves = jnp.concatenate([re * cos - im * sin, im * cos + re * sin], axis=0)
                    row = (2 * w + j) * 16
                    operand_ref[b, row : row + 16, plane * LANES : (plane + 1) * LANES] = waves.astype(BF16)


def on_cells(planes, inverse_ref, operand_ref, point_ref, back, body):
    depth = 4
    dims = (((1,), (1 if back else 0,)), ((), ()))
    for block in range(H // 2 // depth):
        rows = slice(block * depth * G, (block + 1) * depth * G)
        even = jnp.dot(inverse_ref[0, rows], operand_ref[0], preferred_element_type=F32)
        odd = jnp.dot(inverse_ref[1, rows], operand_ref[1], preferred_element_type=F32)
        for side in range(2):
            first = block * depth + side * (H // 2)
            cells = jnp.concatenate([cell_tiles(planes, first + i) for i in range(depth)], axis=0)
            local = lax.dot_general(cells, point_ref[...], dims, preferred_element_type=F32)
            total = local + (even - odd if side else even + odd)
            for i in range(depth):
                for plane in range(2):
                    body(
                        plane,
                        first + i,
                        total[i * G : (i + 1) * G, plane * LANES : (plane + 1) * LANES],
                    )


def gelu_slope(values):
    normal_cdf = 0.5 * (1.0 + lax.erf(values * 0.7071067811865476))
    density = jnp.exp(-0.5 * values * values) * 0.3989422804014327
    return normal_cdf + values * density


def spread_point(point_ref, point):
    low = low_lanes(C)
    twice = jnp.concatenate([point_ref[...], point_ref[...]], axis=1).astype(F32)
    none = jnp.zeros((LANES, LANES), BF16)
    both = jnp.concatenate(
        [jnp.where(low, twice, 0.0), jnp.where(low, 0.0, twice)], axis=0
    ).astype(BF16)
    point[:LANES, :LANES] = both
    point[:LANES, LANES:] = none
    point[LANES:, :LANES] = none
    point[LANES:, LANES:] = both


class Pass:
    def __init__(self, backward, buffers, final, sems, shared):
        self.backward, self.shared = backward, shared
        self.sent, self.arrived = buffers[0:2]
        self.modes_out, self.modes_in, self.mixed_out, self.mixed_in = buffers[2:6]
        self.planes_out = buffers[6]
        by_space = lambda ref: lambda peer, s: ref.at[peer, s]
        by_dp = lambda ref: lambda peer, s: ref.at[s, peer]
        self.to_modes = Exchange("space", SPACE, by_space(self.sent), by_space(self.arrived), sems[0:3])
        self.to_weights = Exchange("dp", DP, by_dp(self.modes_out), by_dp(self.modes_in), sems[3:6])
        self.from_weights = Exchange("dp", DP, by_dp(self.mixed_out), by_dp(self.mixed_in), sems[6:9])
        self.to_planes = Exchange("space", SPACE, by_space(self.planes_out), final, sems[9:12], (2, 3) if backward else ())

    def modes(self, s):
        to_modes, _, turn, _, rows, _, _ = self.shared
        self.to_modes.arrive(2 * s)
        self.to_modes.arrive(2 * s + 1)
        modes_of_sample(s, self.arrived, to_modes, turn, rows, self.modes_out)
        self.to_weights.start(s)

    def mix(self, s):
        _, _, _, wide, rows, mixed_rows, _ = self.shared
        self.to_weights.arrive(s)
        mix_sample(s, self.backward, self.modes_in, wide, rows, mixed_rows, self.mixed_out)
        self.from_weights.start(s)

    def planes(self, s):
        _, to_planes, _, _, rows, _, planes = self.shared
        self.from_weights.arrive(s)
        planes_of_sample(s, self.mixed_in, to_planes, rows, planes, self.planes_out)

    def leave(self):
        for exchange in (self.to_modes, self.to_weights, self.from_weights, self.to_planes):
            exchange.leave()


N_TABLES = 7


def layer_kernel(*refs):
    refs = list(refs)

    def take(count):
        taken = refs[:count]
        del refs[:count]
        return taken

    field_hbm, cotangent_hbm, point_ref, bias_ref = take(4)
    tables_hbm = take(N_TABLES)
    pre_grad_hbm, done_hbm, returned, weight_grad = take(4)
    field, cotangent = take(2)
    tables = take(N_TABLES)
    forward_buffers = take(8)
    backward_buffers = take(8)
    point, wide, rows, mixed_rows, planes, operand = take(6)
    came, came_back = forward_buffers[7], backward_buffers[7]
    field_sem, cotangent_sem, out_sem, table_sem = take(4)
    forward_sems, backward_sems = take(12), take(12)
    weight, grid, inverse, to_modes, to_planes, factors, turn = tables

    def load(s, pair, source, target, sems):
        return pltpu.make_async_copy(
            source.at[s, pl.ds(2 * pair, 2)], target.at[s, pl.ds(2 * pair, 2)], sems.at[s, pair]
        )

    def keep(s, pair):
        source, target = (cotangent, pre_grad_hbm) if s else (field, done_hbm)
        return pltpu.make_async_copy(
            source.at[s, pl.ds(2 * pair, 2)], target.at[pl.ds(2 * pair, 2)], out_sem.at[s, pair]
        )

    def each_pair(body):
        def step(pair, carry):
            body(pair)
            return carry

        lax.fori_loop(0, PAIRS, step, 0)

    def table_copy(i):
        return pltpu.make_async_copy(tables_hbm[i], tables[i], table_sem.at[i])

    barrier = greet()
    table_copy(1).start()
    table_copy(5).start()
    each_pair(lambda pair: load(0, pair, field_hbm, field, field_sem).start())
    shared = (to_modes, to_planes, turn, wide, rows, mixed_rows, planes)
    ahead = Pass(
        False, forward_buffers[:7], lambda peer, c: came.at[peer, c], forward_sems, shared
    )
    back = Pass(
        True,
        backward_buffers[:7],
        lambda peer, c: returned.at[peer, c - 2] if c >= 2 else came_back.at[peer, c],
        backward_sems,
        shared,
    )

    def each_of_half(body):
        def step(inner, carry):
            body(inner)
            return carry

        lax.fori_loop(0, 2, step, 0)

    def forward(s, half):
        def body(inner):
            pair = 2 * half + inner
            load(s, pair, field_hbm, field, field_sem).wait()
            here = (field[s, 2 * pair], field[s, 2 * pair + 1])
            forward_pair(grid, factors.at[0], here, planes, inner)

        each_of_half(body)
        store_forward(planes, ahead.sent, 2 * s + half)

    def middle(s, half):
        bias = jnp.concatenate([bias_ref[...], bias_ref[...]], axis=1)
        ahead.to_planes.arrive(2 * s + half)

        def body(inner):
            pair = 2 * half + inner
            load(s, pair, cotangent_hbm, cotangent, cotangent_sem).wait()
            inverse_operand(
                lambda w, plane, part: came[w, 2 * s + half, 2 * inner + plane, part],
                factors.at[1],
                operand,
            )

            def cell(plane, h, value):
                lanes = slice(h * LANES, (h + 1) * LANES)
                upstream = cotangent[s, 2 * pair + plane, :, lanes].astype(F32)
                grad = upstream * gelu_slope(value + bias)
                cotangent[s, 2 * pair + plane, :, lanes] = grad.astype(BF16)

            here = (field[s, 2 * pair], field[s, 2 * pair + 1])
            on_cells(here, inverse, operand, point, False, cell)
            if s:
                keep(s, pair).start()
            there = (cotangent[s, 2 * pair], cotangent[s, 2 * pair + 1])
            forward_pair(grid, factors.at[1], there, planes, inner)

        each_of_half(body)
        store_forward(planes, back.sent, 2 * s + half)

    def last(half):
        back.to_planes.arrive(half)

        def body(inner):
            pair = 2 * half + inner
            inverse_operand(
                lambda w, plane, part: came_back[w, half, 2 * inner + plane, part], factors.at[0], operand
            )

            def cell(plane, h, value):
                field[0, 2 * pair + plane, :, h * LANES : (h + 1) * LANES] = value.astype(BF16)

            here = (cotangent[0, 2 * pair], cotangent[0, 2 * pair + 1])
            on_cells(here, inverse, operand, point, True, cell)
            keep(0, pair).start()

        each_of_half(body)

    table_copy(1).wait()
    table_copy(5).wait()
    forward(0, 0)
    pl.semaphore_wait(barrier, SPACE + DP - 2)
    ahead.to_modes.start(0)
    each_pair(lambda pair: load(1, pair, field_hbm, field, field_sem).start())
    for i in (0, 2, 3, 4, 6):
        table_copy(i).start()
    forward(0, 1)
    ahead.to_modes.start(1)
    forward(1, 0)
    for i in (0, 2, 3, 4, 6):
        table_copy(i).wait()
    ahead.to_modes.start(2, after=0)
    for s in range(HERE):
        each_pair(lambda pair: load(s, pair, cotangent_hbm, cotangent, cotangent_sem).start())
    forward(1, 1)
    widen(weight, wide)
    spread_point(point_ref, point)
    ahead.to_modes.start(3, after=1)
    ahead.modes(0)
    ahead.mix(0)
    ahead.modes(1)
    ahead.planes(0)
    ahead.to_planes.start(0)
    ahead.mix(1)
    ahead.to_planes.start(1, after=0)
    ahead.planes(1)
    ahead.to_planes.start(2)
    ahead.to_planes.start(3)
    middle(0, 0)
    back.to_modes.start(0)
    middle(0, 1)
    back.to_modes.start(1)
    middle(1, 0)
    back.to_modes.start(2)
    middle(1, 1)
    back.to_modes.start(3)
    back.modes(0)
    back.mix(0)
    back.modes(1)
    back.planes(0)
    back.to_planes.start(0)
    back.to_planes.start(1)
    back.mix(1)
    weight_gradient(ahead.modes_in, back.modes_in, rows, mixed_rows, weight_grad)
    back.planes(1)
    back.to_planes.start(2)
    back.to_planes.start(3)
    last(0)
    last(1)
    back.to_planes.arrive(2)
    back.to_planes.arrive(3)
    ahead.leave()
    back.leave()
    for s in range(HERE):
        each_pair(lambda pair: keep(s, pair).wait())


def final_kernel(
    returned,
    pre_grad_hbm,
    done_hbm,
    weight_grad_hbm,
    inverse,
    factors,
    point_ref,
    out_hbm,
    kept_hbm,
    came,
    pre_grad,
    out,
    done,
    weight_grad,
    operand,
    point,
    came_sem,
    pre_grad_sem,
    out_sem,
    done_sem,
    copy_sem,
):
    def came_copy(half):
        return pltpu.make_async_copy(returned.at[:, half], came.at[half], came_sem.at[half])

    def two(pair):
        return pl.ds(2 * pair, 2)

    def load(pair):
        return pltpu.make_async_copy(
            pre_grad_hbm.at[two(pair)], pre_grad.at[two(pair)], pre_grad_sem.at[pair]
        )

    def keep(pair):
        return pltpu.make_async_copy(out.at[two(pair)], out_hbm.at[1, two(pair)], out_sem.at[pair])

    def fetch(pair):
        return pltpu.make_async_copy(done_hbm.at[two(pair)], done.at[two(pair)], done_sem.at[pair])

    def pass_on(pair):
        return pltpu.make_async_copy(done.at[two(pair)], out_hbm.at[0, two(pair)], done_sem.at[pair])

    weight_in = pltpu.make_async_copy(weight_grad_hbm, weight_grad, copy_sem.at[0])
    weight_out = pltpu.make_async_copy(weight_grad, kept_hbm, copy_sem.at[1])
    came_copy(0).start()
    load(0).start()
    load(1).start()
    spread_point(point_ref, point)
    for half in range(2):
        came_copy(half).wait()
        if half == 0:
            came_copy(1).start()
            for pair in (2, 3):
                load(pair).start()
            for pair in range(PAIRS):
                fetch(pair).start()
            weight_in.start()

        def step(inner, carry):
            pair = 2 * half + inner
            load(pair).wait()
            inverse_operand(
                lambda w, plane, part: came[half, w, 2 * inner + plane, part], factors.at[0], operand
            )

            def cell(plane, h, value):
                out[2 * pair + plane, :, h * LANES : (h + 1) * LANES] = value.astype(BF16)

            here = (pre_grad[2 * pair], pre_grad[2 * pair + 1])
            on_cells(here, inverse, operand, point, True, cell)
            keep(pair).start()
            fetch(pair).wait()
            pass_on(pair).start()
            return carry

        lax.fori_loop(0, 2, step, 0)
        if half == 0:
            weight_in.wait()
            weight_out.start()
    for pair in range(PAIRS):
        keep(pair).wait()
        pass_on(pair).wait()
    weight_out.wait()


SENT = jax.ShapeDtypeStruct((SPACE, 2 * HERE, 8, 16, LANES), BF16)
MODES = jax.ShapeDtypeStruct((HERE, DP, 32, LANES), BF16)
RETURNED = jax.ShapeDtypeStruct((SPACE, 2 * HERE, 4, 32, LANES), BF16)
ONE_RETURNED = jax.ShapeDtypeStruct((SPACE, 2, 4, 32, LANES), BF16)
ROWS_SCRATCH = pltpu.VMEM((DP * 32, LANES), F32)
OPERAND_SCRATCH = pltpu.VMEM((2, K * K, 2 * LANES), BF16)
ANYWHERE = pl.BlockSpec(memory_space=pl.ANY)
IN_VMEM = pl.BlockSpec(memory_space=pltpu.VMEM)
SENT_SCRATCH = pltpu.VMEM((SPACE * 256, LANES), F32)


def on_device(field, cotangent, spectral_weight, point_weight, bias):
    table = grid_table()
    tables = [
        spectral_weight,
        jnp.asarray(bf16_table(table)),
        jnp.asarray(bf16_table(table.transpose(0, 2, 1))),
        jnp.asarray(bf16_table(plane_table())),
        jnp.asarray(bf16_table(plane_inverse_table())),
        jnp.asarray(np.stack([cell_factor(False), cell_factor(True)])),
        jnp.asarray(plane_factor()),
    ]
    weight_grad_type = jax.ShapeDtypeStruct(spectral_weight.shape, F32)
    grid_type = jax.ShapeDtypeStruct(field.shape, BF16)
    buffers = [pltpu.VMEM(SENT.shape, BF16)] * 2
    buffers += [pltpu.VMEM(MODES.shape, BF16)] * 4
    buffers += [pltpu.VMEM(RETURNED.shape, BF16)]
    sems = []
    for chunks, size in ((2 * HERE, SPACE), (HERE, DP), (HERE, DP), (2 * HERE, SPACE)):
        sems += [
            pltpu.SemaphoreType.DMA((chunks, size)),
            pltpu.SemaphoreType.DMA((chunks, size)),
            pltpu.SemaphoreType.DMA((chunks,)),
        ]
    sample_type = jax.ShapeDtypeStruct(field.shape[1:], BF16)
    pre_grad, done, arrived, weight_grad = pl.pallas_call(
        layer_kernel,
        in_specs=[ANYWHERE, ANYWHERE, IN_VMEM, IN_VMEM] + [ANYWHERE] * N_TABLES,
        out_specs=[ANYWHERE, ANYWHERE, ANYWHERE, IN_VMEM],
        out_shape=[sample_type, sample_type, ONE_RETURNED, weight_grad_type],
        scratch_shapes=[pltpu.VMEM(field.shape, BF16)] * 2
        + [pltpu.VMEM(table.shape, table.dtype) for table in tables]
        + buffers
        + [pltpu.VMEM(RETURNED.shape, BF16)]
        + buffers
        + [pltpu.VMEM(ONE_RETURNED.shape, BF16)]
        + [
            pltpu.VMEM((2 * LANES, 2 * LANES), BF16),
            pltpu.VMEM((32, LANES, LANES), BF16),
            ROWS_SCRATCH,
            ROWS_SCRATCH,
            SENT_SCRATCH,
            OPERAND_SCRATCH,
        ]
        + [pltpu.SemaphoreType.DMA((HERE, PAIRS))] * 3
        + [pltpu.SemaphoreType.DMA((N_TABLES,))]
        + sems
        + sems,
        compiler_params=pltpu.CompilerParams(
            vmem_limit_bytes=56 * 1024 * 1024, collective_id=0, has_side_effects=True
        ),
        name="layer",
    )(field, cotangent, point_weight, bias[None, :], *tables)
    field_grad, weight_grad = pl.pallas_call(
        final_kernel,
        in_specs=[ANYWHERE] * 4 + [IN_VMEM] * 3,
        out_specs=[ANYWHERE, ANYWHERE],
        out_shape=[grid_type, weight_grad_type],
        scratch_shapes=[
            pltpu.VMEM((2, SPACE, 4, 32, LANES), BF16),
            pltpu.VMEM(sample_type.shape, BF16),
            pltpu.VMEM(sample_type.shape, BF16),
            pltpu.VMEM(sample_type.shape, BF16),
            pltpu.VMEM(spectral_weight.shape, F32),
            OPERAND_SCRATCH,
            pltpu.VMEM((2 * LANES, 2 * LANES), BF16),
            pltpu.SemaphoreType.DMA((2,)),
            pltpu.SemaphoreType.DMA((PAIRS,)),
            pltpu.SemaphoreType.DMA((PAIRS,)),
            pltpu.SemaphoreType.DMA((PAIRS,)),
            pltpu.SemaphoreType.DMA((2,)),
        ],
        compiler_params=pltpu.CompilerParams(vmem_limit_bytes=60 * 1024 * 1024),
        name="final",
    )(arrived, pre_grad, done, weight_grad, tables[2], tables[5], point_weight)
    return (field_grad, weight_grad)


def solution(mesh):
    return jax.shard_map(
        on_device,
        mesh=mesh,
        in_specs=(
            P("dp", "space", None, None),
            P("dp", "space", None, None),
            P("dp", "space", None, None),
            P(),
            P(),
        ),
        out_specs=(P("dp", "space", None, None), P("dp", "space", None, None)),
        check_vma=False,
    )
```

```python
import jax
import jax.numpy as jnp
import ml_dtypes
import numpy as np
from jax import lax
from jax.experimental import pallas as pl
from jax.experimental.pallas import tpu as pltpu
from jax.sharding import PartitionSpec as P

C = 64
K = 16
G = 64
H = G // 2
LANES = 2 * C
PLANES = 8
PAIRS = PLANES // 2
SPACE = 8
DP = 16
HERE = 2
SAMPLES = 32
F32 = jnp.float32
BF16 = jnp.bfloat16


def cosine(turns):
    return np.cos(2.0 * np.pi * (turns % G) / G)


def sine(turns):
    return np.sin(2.0 * np.pi * (turns % G) / G)


def grid_table():
    freq = np.arange(K)
    signed = np.where(freq < K // 2, freq, freq - K)
    k3 = freq.reshape(K // 2, 2).T
    turns = (
        signed[None, :, None, None, None] * np.arange(G)
        + k3[:, None, :, None, None] * 2 * np.arange(H // 2)[:, None]
    )
    table = np.stack([cosine(turns), -sine(turns)], axis=2) / G
    return table.reshape(2, K * K, G * H // 2)


def plane_table():
    freq = np.arange(K)
    signed = np.where(freq < K // 2, freq, freq - K)
    planes = (PLANES * np.arange(SPACE)[:, None] + 2 * np.arange(PAIRS)[None, :]).reshape(SPACE, 2, 2)
    turns = signed[:, None, None, None] * planes[None]
    cos, sin = cosine(turns) / 8.0, sine(turns) / 8.0
    table = np.zeros((2, 2, 2, K, SPACE, 2, 2, 2, 2, 2))
    for b in range(2):
        for j in range(2):
            table[b, j, 0, :, :, :, b, j, 0] = cos
            table[b, j, 0, :, :, :, b, j, 1] = sin
            table[b, j, 1, :, :, :, b, j, 0] = -sin
            table[b, j, 1, :, :, :, b, j, 1] = cos
    return table.reshape(8 * K, SPACE * 32)


def plane_inverse_table():
    freq = np.arange(K)
    signed = np.where(freq < K // 2, freq, freq - K)
    turns = (PLANES * np.arange(SPACE)[:, None, None] + np.arange(PLANES)[None, :, None]) * signed
    cos, sin = cosine(turns) / 8.0, sine(turns) / 8.0
    table = np.zeros((SPACE, 2, PLANES, 2, K))
    table[:, 0, :, 0] = cos
    table[:, 0, :, 1] = -sin
    table[:, 1, :, 0] = sin
    table[:, 1, :, 1] = cos
    return table.reshape(SPACE * 2 * PLANES, 2 * K)


def cell_factor(weighted):
    freq = np.arange(K)
    weight = np.where(freq == 0, 1.0, 2.0) if weighted else np.ones(K)
    out = np.zeros((2, K, 2, C))
    out[0, :, 0] = weight[:, None]
    out[0, :, 1] = (weight * cosine(freq))[:, None]
    out[1, :, 1] = (weight * sine(freq))[:, None]
    out = out.reshape(2, K // 2, 2, LANES).transpose(2, 0, 1, 3)
    return np.ascontiguousarray(out, dtype=np.float32)


def plane_factor():
    freq = np.arange(K)
    signed = np.where(freq < K // 2, freq, freq - K)
    out = np.zeros((2, K, 2, C))
    out[0, :, 0] = 1.0
    out[0, :, 1] = cosine(signed)[:, None]
    out[1, :, 1] = sine(signed)[:, None]
    return out.reshape(2, K, LANES).astype(np.float32)


def bf16_table(values):
    return np.asarray(values, np.float32).astype(ml_dtypes.bfloat16)


def low_lanes(rows):
    return lax.broadcasted_iota(jnp.int32, (rows, LANES), 1) < C


def swap_halves(tile):
    return pltpu.roll(tile, C, 1)


def fold_halves(low, first, second):
    return jnp.where(low, first, second) + swap_halves(jnp.where(low, second, first))


def cell_tiles(planes, h):
    lanes = slice(h * LANES, (h + 1) * LANES)
    return jnp.concatenate([plane[:, lanes] for plane in planes], axis=1)


def forward_pair(table_ref, factor_ref, planes, scratch, pair):
    low = low_lanes(K // 2)
    for b in range(2):
        parts = []
        for h in range(H // 2):
            near, far = cell_tiles(planes, h), cell_tiles(planes, h + H // 2)
            parts.append(near - far if b else near + far)
        modes = jnp.dot(
            table_ref[b], jnp.concatenate(parts, axis=0), preferred_element_type=F32
        )
        cos, sin = factor_ref[b, 0], factor_ref[b, 1]
        for j2 in range(K):
            halves = ([], [])
            for plane in range(2):
                lanes = slice(plane * LANES, (plane + 1) * LANES)
                real = modes[j2 * K : j2 * K + 8, lanes]
                imag = modes[j2 * K + 8 : j2 * K + 16, lanes]
                halves[0].append(real * cos + imag * sin)
                halves[1].append(imag * cos - real * sin)
            for q in range(2):
                start = (j2 // 2) * 128 + b * 8 + (j2 % 2) * 4 + q * 2 + pair
                scratch[pl.ds(start, 8, stride=16), :] = fold_halves(low, *halves[q])


def store_forward(scratch, out, chunk):
    for p in range(SPACE):
        out[p, chunk] = scratch[p * 128 : (p + 1) * 128, :].reshape(8, 16, LANES).astype(BF16)


def modes_of_sample(s, arrived, table_ref, factor_ref, rows, out):
    low = low_lanes(K)
    cos, sin = factor_ref[0], factor_ref[1]
    operand = jnp.concatenate(
        [
            jnp.concatenate(
                [arrived[w, 2 * s + half, k] for w in range(SPACE) for half in range(2)], axis=0
            )
            for k in range(8)
        ],
        axis=1,
    )
    modes = jnp.dot(table_ref[...], operand, preferred_element_type=F32)
    for k in range(8):
        lanes = slice(k * LANES, (k + 1) * LANES)
        for b in range(2):
            for j in range(2):
                row = (b * 2 + j) * 32
                real = modes[row : row + K, lanes]
                imag = modes[row + K : row + 2 * K, lanes]
                rows[pl.ds((2 * k + b) * 2 + j, K, stride=32), :] = fold_halves(
                    low, real * cos + imag * sin, imag * cos - real * sin
                )
    out[s] = rows[...].reshape(DP, 32, LANES).astype(BF16)


def widen(weight_ref, wide):
    low = low_lanes(C)
    for item in range(32):
        top = weight_ref[item // 2, item % 2]
        turned = swap_halves(top.astype(F32))
        wide[item, :C] = top
        wide[item, C:] = jnp.where(low, -turned, turned).astype(BF16)


def mix_sample(s, backward, modes, wide, rows, mixed_rows, out):
    rows[...] = modes[s].reshape(DP * 32, LANES).astype(F32)
    dims = (((1,), (1,)), ((), ())) if backward else (((1,), (0,)), ((), ()))
    for item in range(32):
        here = pl.ds(item, DP, stride=32)
        mixed_rows[here, :] = lax.dot_general(
            rows[here, :].astype(BF16), wide[item], dims, preferred_element_type=F32
        )
    out[s] = mixed_rows[...].reshape(DP, 32, LANES).astype(BF16)


def weight_gradient(field_modes, grad_modes, rows, mixed_rows, weight_grad_ref):
    low = low_lanes(C)
    for s in range(HERE):
        rows[...] = field_modes[s].reshape(DP * 32, LANES).astype(F32)
        mixed_rows[...] = grad_modes[s].reshape(DP * 32, LANES).astype(F32)
        for item in range(32):
            here = pl.ds(item, DP, stride=32)
            outer = lax.dot_general(
                rows[here, :].astype(BF16),
                mixed_rows[here, :].astype(BF16),
                (((0,), (0,)), ((), ())),
                preferred_element_type=F32,
            )
            turned = swap_halves(outer[C:])
            term = (outer[:C] + jnp.where(low, turned, -turned)) * (1.0 / SAMPLES)
            if s == 0:
                weight_grad_ref[item // 2, item % 2] = term
            else:
                weight_grad_ref[item // 2, item % 2] += term


def planes_of_sample(s, mixed, table_ref, rows, planes, out):
    low = low_lanes(K)
    rows[...] = mixed[s].reshape(DP * 32, LANES).astype(F32)
    columns = []
    for k3 in range(K):
        first = rows[pl.ds(k3 * 2, K, stride=32), :]
        second = rows[pl.ds(k3 * 2 + 1, K, stride=32), :]
        real = jnp.where(low, first, swap_halves(second))
        imag = jnp.where(low, swap_halves(first), second)
        columns.append(jnp.concatenate([real, imag], axis=0).astype(BF16))
    partial = jnp.dot(
        table_ref[...], jnp.concatenate(columns, axis=1), preferred_element_type=F32
    )
    for p in range(SPACE):
        for r in range(2):
            row = (p * 2 + r) * PLANES
            for k3 in range(K):
                start = p * 256 + (k3 % 2) * 16 + r * 8 + k3 // 2
                planes[pl.ds(start, PLANES, stride=32), :] = partial[
                    row : row + PLANES, k3 * LANES : (k3 + 1) * LANES
                ]
        for half in range(2):
            start = p * 256 + half * 128
            out[p, 2 * s + half] = planes[start : start + 128, :].reshape(4, 32, LANES).astype(BF16)


class Exchange:
    def __init__(self, axis, size, source, target, sems, far=()):
        self.axis, self.size, self.source, self.target = axis, size, source, target
        self.send, self.recv, self.own = sems
        self.me = lax.axis_index(axis)
        self.far = far
        self.away = []

    def remote(self, s, slot, peer):
        return pltpu.make_async_remote_copy(
            src_ref=self.source(peer, s),
            dst_ref=self.target(slot, s),
            send_sem=self.send.at[s, peer],
            recv_sem=self.recv.at[s, slot],
            device_id={self.axis: peer},
            device_id_type=pl.DeviceIdType.MESH,
        )

    def local(self, s):
        return pltpu.make_async_copy(
            self.source(self.me, s), self.target(self.me, s), self.own.at[s]
        )

    def peers(self, body):
        def step(offset, carry):
            body(lax.rem(self.me + offset, self.size))
            return carry

        lax.fori_loop(1, self.size, step, 0)

    def start(self, s, after=None):
        def one(peer):
            if after is not None:
                self.remote(after, self.me, peer).wait_send()
            self.remote(s, self.me, peer).start()

        self.peers(one)
        if s in self.far:
            self.local(s).start()
        else:
            self.target(self.me, s)[...] = self.source(self.me, s)[...]
        if after is not None:
            self.away.remove(after)
        self.away.append(s)

    def arrive(self, s):
        self.peers(lambda peer: self.remote(s, peer, peer).wait_recv())
        if s in self.far:
            self.local(s).wait()

    def leave(self):
        for s in self.away:
            self.peers(lambda peer: self.remote(s, self.me, peer).wait_send())


def greet():
    barrier = pltpu.get_barrier_semaphore()
    for axis, size in (("space", SPACE), ("dp", DP)):
        me = lax.axis_index(axis)

        def step(offset, carry):
            pl.semaphore_signal(
                barrier,
                inc=1,
                device_id={axis: lax.rem(me + offset, size)},
                device_id_type=pl.DeviceIdType.MESH,
            )
            return carry

        lax.fori_loop(1, size, step, 0)
    return barrier


def inverse_operand(tile_of, factor_ref, operand_ref):
    low = low_lanes(8)
    for plane in range(2):
        for b in range(2):
            cos, sin = factor_ref[b, 0], factor_ref[b, 1]
            for w in range(SPACE):
                tile = tile_of(w, plane, slice(b * 16, (b + 1) * 16)).astype(F32)
                real, imag = tile[:8], tile[8:]
                real_turned, imag_turned = swap_halves(real), swap_halves(imag)
                for j in range(2):
                    if j == 0:
                        re = jnp.where(low, real, real_turned)
                        im = jnp.where(low, imag, imag_turned)
                    else:
                        re = jnp.where(low, real_turned, real)
                        im = jnp.where(low, imag_turned, imag)
                    waves = jnp.concatenate([re * cos - im * sin, im * cos + re * sin], axis=0)
                    row = (2 * w + j) * 16
                    operand_ref[b, row : row + 16, plane * LANES : (plane + 1) * LANES] = waves.astype(BF16)


def on_cells(planes, inverse_ref, operand_ref, point_ref, back, body):
    depth = 4
    dims = (((1,), (1 if back else 0,)), ((), ()))
    for block in range(H // 2 // depth):
        rows = slice(block * depth * G, (block + 1) * depth * G)
        even = jnp.dot(inverse_ref[0, rows], operand_ref[0], preferred_element_type=F32)
        odd = jnp.dot(inverse_ref[1, rows], operand_ref[1], preferred_element_type=F32)
        for side in range(2):
            first = block * depth + side * (H // 2)
            cells = jnp.concatenate([cell_tiles(planes, first + i) for i in range(depth)], axis=0)
            local = lax.dot_general(cells, point_ref[...], dims, preferred_element_type=F32)
            total = local + (even - odd if side else even + odd)
            for i in range(depth):
                for plane in range(2):
                    body(
                        plane,
                        first + i,
                        total[i * G : (i + 1) * G, plane * LANES : (plane + 1) * LANES],
                    )


def gelu_slope(values):
    normal_cdf = 0.5 * (1.0 + lax.erf(values * 0.7071067811865476))
    density = jnp.exp(-0.5 * values * values) * 0.3989422804014327
    return normal_cdf + values * density


def spread_point(point_ref, point):
    low = low_lanes(C)
    twice = jnp.concatenate([point_ref[...], point_ref[...]], axis=1).astype(F32)
    none = jnp.zeros((LANES, LANES), BF16)
    both = jnp.concatenate(
        [jnp.where(low, twice, 0.0), jnp.where(low, 0.0, twice)], axis=0
    ).astype(BF16)
    point[:LANES, :LANES] = both
    point[:LANES, LANES:] = none
    point[LANES:, :LANES] = none
    point[LANES:, LANES:] = both


class Pass:
    def __init__(self, backward, buffers, final, sems, shared):
        self.backward, self.shared = backward, shared
        self.sent, self.arrived = buffers[0:2]
        self.modes_out, self.modes_in, self.mixed_out, self.mixed_in = buffers[2:6]
        self.planes_out = buffers[6]
        by_space = lambda ref: lambda peer, s: ref.at[peer, s]
        by_dp = lambda ref: lambda peer, s: ref.at[s, peer]
        self.to_modes = Exchange("space", SPACE, by_space(self.sent), by_space(self.arrived), sems[0:3])
        self.to_weights = Exchange("dp", DP, by_dp(self.modes_out), by_dp(self.modes_in), sems[3:6])
        self.from_weights = Exchange("dp", DP, by_dp(self.mixed_out), by_dp(self.mixed_in), sems[6:9])
        self.to_planes = Exchange("space", SPACE, by_space(self.planes_out), final, sems[9:12], (2, 3) if backward else ())

    def modes(self, s):
        to_modes, _, turn, _, rows, _, _ = self.shared
        self.to_modes.arrive(2 * s)
        self.to_modes.arrive(2 * s + 1)
        modes_of_sample(s, self.arrived, to_modes, turn, rows, self.modes_out)
        self.to_weights.start(s)

    def mix(self, s):
        _, _, _, wide, rows, mixed_rows, _ = self.shared
        self.to_weights.arrive(s)
        mix_sample(s, self.backward, self.modes_in, wide, rows, mixed_rows, self.mixed_out)
        self.from_weights.start(s)

    def planes(self, s):
        _, to_planes, _, _, rows, _, planes = self.shared
        self.from_weights.arrive(s)
        planes_of_sample(s, self.mixed_in, to_planes, rows, planes, self.planes_out)

    def leave(self):
        for exchange in (self.to_modes, self.to_weights, self.from_weights, self.to_planes):
            exchange.leave()


N_TABLES = 7


def layer_kernel(*refs):
    refs = list(refs)

    def take(count):
        taken = refs[:count]
        del refs[:count]
        return taken

    field_hbm, cotangent_hbm, point_ref, bias_ref = take(4)
    tables_hbm = take(N_TABLES)
    pre_grad_hbm, done_hbm, returned, weight_grad = take(4)
    field, cotangent = take(2)
    tables = take(N_TABLES)
    forward_buffers = take(8)
    backward_buffers = take(8)
    point, wide, rows, mixed_rows, planes, operand = take(6)
    came, came_back = forward_buffers[7], backward_buffers[7]
    field_sem, cotangent_sem, out_sem, table_sem = take(4)
    forward_sems, backward_sems = take(12), take(12)
    weight, grid, inverse, to_modes, to_planes, factors, turn = tables

    def load(s, pair, source, target, sems):
        return pltpu.make_async_copy(
            source.at[s, pl.ds(2 * pair, 2)], target.at[s, pl.ds(2 * pair, 2)], sems.at[s, pair]
        )

    def keep(s, pair):
        source, target = (cotangent, pre_grad_hbm) if s else (field, done_hbm)
        return pltpu.make_async_copy(
            source.at[s, pl.ds(2 * pair, 2)], target.at[pl.ds(2 * pair, 2)], out_sem.at[s, pair]
        )

    def each_pair(body):
        def step(pair, carry):
            body(pair)
            return carry

        lax.fori_loop(0, PAIRS, step, 0)

    def table_copy(i):
        return pltpu.make_async_copy(tables_hbm[i], tables[i], table_sem.at[i])

    barrier = greet()
    table_copy(1).start()
    table_copy(5).start()
    each_pair(lambda pair: load(0, pair, field_hbm, field, field_sem).start())
    shared = (to_modes, to_planes, turn, wide, rows, mixed_rows, planes)
    ahead = Pass(
        False, forward_buffers[:7], lambda peer, c: came.at[peer, c], forward_sems, shared
    )
    back = Pass(
        True,
        backward_buffers[:7],
        lambda peer, c: returned.at[peer, c - 2] if c >= 2 else came_back.at[peer, c],
        backward_sems,
        shared,
    )

    def each_of_half(body):
        def step(inner, carry):
            body(inner)
            return carry

        lax.fori_loop(0, 2, step, 0)

    def forward(s, half):
        def body(inner):
            pair = 2 * half + inner
            load(s, pair, field_hbm, field, field_sem).wait()
            here = (field[s, 2 * pair], field[s, 2 * pair + 1])
            forward_pair(grid, factors.at[0], here, planes, inner)

        each_of_half(body)
        store_forward(planes, ahead.sent, 2 * s + half)

    def middle(s, half):
        bias = jnp.concatenate([bias_ref[...], bias_ref[...]], axis=1)
        ahead.to_planes.arrive(2 * s + half)

        def body(inner):
            pair = 2 * half + inner
            load(s, pair, cotangent_hbm, cotangent, cotangent_sem).wait()
            inverse_operand(
                lambda w, plane, part: came[w, 2 * s + half, 2 * inner + plane, part],
                factors.at[1],
                operand,
            )

            def cell(plane, h, value):
                lanes = slice(h * LANES, (h + 1) * LANES)
                upstream = cotangent[s, 2 * pair + plane, :, lanes].astype(F32)
                grad = upstream * gelu_slope(value + bias)
                cotangent[s, 2 * pair + plane, :, lanes] = grad.astype(BF16)

            here = (field[s, 2 * pair], field[s, 2 * pair + 1])
            on_cells(here, inverse, operand, point, False, cell)
            if s:
                keep(s, pair).start()
            there = (cotangent[s, 2 * pair], cotangent[s, 2 * pair + 1])
            forward_pair(grid, factors.at[1], there, planes, inner)

        each_of_half(body)
        store_forward(planes, back.sent, 2 * s + half)

    def last(half):
        back.to_planes.arrive(half)

        def body(inner):
            pair = 2 * half + inner
            inverse_operand(
                lambda w, plane, part: came_back[w, half, 2 * inner + plane, part], factors.at[0], operand
            )

            def cell(plane, h, value):
                field[0, 2 * pair + plane, :, h * LANES : (h + 1) * LANES] = value.astype(BF16)

            here = (cotangent[0, 2 * pair], cotangent[0, 2 * pair + 1])
            on_cells(here, inverse, operand, point, True, cell)
            keep(0, pair).start()

        each_of_half(body)

    table_copy(1).wait()
    table_copy(5).wait()
    forward(0, 0)
    pl.semaphore_wait(barrier, SPACE + DP - 2)
    ahead.to_modes.start(0)
    each_pair(lambda pair: load(1, pair, field_hbm, field, field_sem).start())
    for i in (0, 2, 3, 4, 6):
        table_copy(i).start()
    forward(0, 1)
    ahead.to_modes.start(1)
    forward(1, 0)
    for i in (0, 2, 3, 4, 6):
        table_copy(i).wait()
    ahead.to_modes.start(2, after=0)
    for s in range(HERE):
        each_pair(lambda pair: load(s, pair, cotangent_hbm, cotangent, cotangent_sem).start())
    forward(1, 1)
    widen(weight, wide)
    spread_point(point_ref, point)
    ahead.to_modes.start(3, after=1)
    ahead.modes(0)
    ahead.mix(0)
    ahead.modes(1)
    ahead.planes(0)
    ahead.to_planes.start(0)
    ahead.mix(1)
    ahead.to_planes.start(1, after=0)
    ahead.planes(1)
    ahead.to_planes.start(2)
    ahead.to_planes.start(3)
    middle(0, 0)
    back.to_modes.start(0)
    middle(0, 1)
    back.to_modes.start(1)
    middle(1, 0)
    back.to_modes.start(2)
    back.modes(0)
    middle(1, 1)
    back.to_modes.start(3)
    back.mix(0)
    back.modes(1)
    back.planes(0)
    back.to_planes.start(0)
    back.to_planes.start(1)
    back.mix(1)
    weight_gradient(ahead.modes_in, back.modes_in, rows, mixed_rows, weight_grad)
    back.planes(1)
    back.to_planes.start(2)
    back.to_planes.start(3)
    last(0)
    last(1)
    back.to_planes.arrive(2)
    back.to_planes.arrive(3)
    ahead.leave()
    back.leave()
    for s in range(HERE):
        each_pair(lambda pair: keep(s, pair).wait())


def final_kernel(
    returned,
    pre_grad_hbm,
    done_hbm,
    weight_grad_hbm,
    inverse,
    factors,
    point_ref,
    out_hbm,
    kept_hbm,
    came,
    pre_grad,
    out,
    done,
    weight_grad,
    operand,
    point,
    came_sem,
    pre_grad_sem,
    out_sem,
    done_sem,
    copy_sem,
):
    def came_copy(half):
        return pltpu.make_async_copy(returned.at[:, half], came.at[half], came_sem.at[half])

    def two(pair):
        return pl.ds(2 * pair, 2)

    def load(pair):
        return pltpu.make_async_copy(
            pre_grad_hbm.at[two(pair)], pre_grad.at[two(pair)], pre_grad_sem.at[pair]
        )

    def keep(pair):
        return pltpu.make_async_copy(out.at[two(pair)], out_hbm.at[1, two(pair)], out_sem.at[pair])

    def fetch(pair):
        return pltpu.make_async_copy(done_hbm.at[two(pair)], done.at[two(pair)], done_sem.at[pair])

    def pass_on(pair):
        return pltpu.make_async_copy(done.at[two(pair)], out_hbm.at[0, two(pair)], done_sem.at[pair])

    weight_in = pltpu.make_async_copy(weight_grad_hbm, weight_grad, copy_sem.at[0])
    weight_out = pltpu.make_async_copy(weight_grad, kept_hbm, copy_sem.at[1])
    for half in range(2):
        came_copy(half).start()
        for pair in (2 * half, 2 * half + 1):
            load(pair).start()
            fetch(pair).start()
    weight_in.start()
    spread_point(point_ref, point)
    for half in range(2):
        came_copy(half).wait()

        def step(inner, carry):
            pair = 2 * half + inner
            load(pair).wait()
            fetch(pair).wait()
            pass_on(pair).start()
            inverse_operand(
                lambda w, plane, part: came[half, w, 2 * inner + plane, part], factors.at[0], operand
            )

            def cell(plane, h, value):
                out[2 * pair + plane, :, h * LANES : (h + 1) * LANES] = value.astype(BF16)

            here = (pre_grad[2 * pair], pre_grad[2 * pair + 1])
            on_cells(here, inverse, operand, point, True, cell)
            keep(pair).start()
            return carry

        lax.fori_loop(0, 2, step, 0)
        if half == 0:
            weight_in.wait()
            weight_out.start()
    for pair in range(PAIRS):
        keep(pair).wait()
        pass_on(pair).wait()
    weight_out.wait()


SENT = jax.ShapeDtypeStruct((SPACE, 2 * HERE, 8, 16, LANES), BF16)
MODES = jax.ShapeDtypeStruct((HERE, DP, 32, LANES), BF16)
RETURNED = jax.ShapeDtypeStruct((SPACE, 2 * HERE, 4, 32, LANES), BF16)
ONE_RETURNED = jax.ShapeDtypeStruct((SPACE, 2, 4, 32, LANES), BF16)
ROWS_SCRATCH = pltpu.VMEM((DP * 32, LANES), F32)
OPERAND_SCRATCH = pltpu.VMEM((2, K * K, 2 * LANES), BF16)
ANYWHERE = pl.BlockSpec(memory_space=pl.ANY)
IN_VMEM = pl.BlockSpec(memory_space=pltpu.VMEM)
SENT_SCRATCH = pltpu.VMEM((SPACE * 256, LANES), F32)


def on_device(field, cotangent, spectral_weight, point_weight, bias):
    table = grid_table()
    tables = [
        spectral_weight,
        jnp.asarray(bf16_table(table)),
        jnp.asarray(bf16_table(table.transpose(0, 2, 1))),
        jnp.asarray(bf16_table(plane_table())),
        jnp.asarray(bf16_table(plane_inverse_table())),
        jnp.asarray(np.stack([cell_factor(False), cell_factor(True)])),
        jnp.asarray(plane_factor()),
    ]
    weight_grad_type = jax.ShapeDtypeStruct(spectral_weight.shape, F32)
    grid_type = jax.ShapeDtypeStruct(field.shape, BF16)
    buffers = [pltpu.VMEM(SENT.shape, BF16)] * 2
    buffers += [pltpu.VMEM(MODES.shape, BF16)] * 4
    buffers += [pltpu.VMEM(RETURNED.shape, BF16)]
    sems = []
    for chunks, size in ((2 * HERE, SPACE), (HERE, DP), (HERE, DP), (2 * HERE, SPACE)):
        sems += [
            pltpu.SemaphoreType.DMA((chunks, size)),
            pltpu.SemaphoreType.DMA((chunks, size)),
            pltpu.SemaphoreType.DMA((chunks,)),
        ]
    sample_type = jax.ShapeDtypeStruct(field.shape[1:], BF16)
    pre_grad, done, arrived, weight_grad = pl.pallas_call(
        layer_kernel,
        in_specs=[ANYWHERE, ANYWHERE, IN_VMEM, IN_VMEM] + [ANYWHERE] * N_TABLES,
        out_specs=[ANYWHERE, ANYWHERE, ANYWHERE, IN_VMEM],
        out_shape=[sample_type, sample_type, ONE_RETURNED, weight_grad_type],
        scratch_shapes=[pltpu.VMEM(field.shape, BF16)] * 2
        + [pltpu.VMEM(table.shape, table.dtype) for table in tables]
        + buffers
        + [pltpu.VMEM(RETURNED.shape, BF16)]
        + buffers
        + [pltpu.VMEM(ONE_RETURNED.shape, BF16)]
        + [
            pltpu.VMEM((2 * LANES, 2 * LANES), BF16),
            pltpu.VMEM((32, LANES, LANES), BF16),
            ROWS_SCRATCH,
            ROWS_SCRATCH,
            SENT_SCRATCH,
            OPERAND_SCRATCH,
        ]
        + [pltpu.SemaphoreType.DMA((HERE, PAIRS))] * 3
        + [pltpu.SemaphoreType.DMA((N_TABLES,))]
        + sems
        + sems,
        compiler_params=pltpu.CompilerParams(
            vmem_limit_bytes=56 * 1024 * 1024, collective_id=0, has_side_effects=True
        ),
        name="layer",
    )(field, cotangent, point_weight, bias[None, :], *tables)
    field_grad, weight_grad = pl.pallas_call(
        final_kernel,
        in_specs=[ANYWHERE] * 4 + [IN_VMEM] * 3,
        out_specs=[ANYWHERE, ANYWHERE],
        out_shape=[grid_type, weight_grad_type],
        scratch_shapes=[
            pltpu.VMEM((2, SPACE, 4, 32, LANES), BF16),
            pltpu.VMEM(sample_type.shape, BF16),
            pltpu.VMEM(sample_type.shape, BF16),
            pltpu.VMEM(sample_type.shape, BF16),
            pltpu.VMEM(spectral_weight.shape, F32),
            OPERAND_SCRATCH,
            pltpu.VMEM((2 * LANES, 2 * LANES), BF16),
            pltpu.SemaphoreType.DMA((2,)),
            pltpu.SemaphoreType.DMA((PAIRS,)),
            pltpu.SemaphoreType.DMA((PAIRS,)),
            pltpu.SemaphoreType.DMA((PAIRS,)),
            pltpu.SemaphoreType.DMA((2,)),
        ],
        compiler_params=pltpu.CompilerParams(vmem_limit_bytes=60 * 1024 * 1024),
        name="final",
    )(arrived, pre_grad, done, weight_grad, tables[2], tables[5], point_weight)
    return (field_grad, weight_grad)


def solution(mesh):
    return jax.shard_map(
        on_device,
        mesh=mesh,
        in_specs=(
            P("dp", "space", None, None),
            P("dp", "space", None, None),
            P("dp", "space", None, None),
            P(),
            P(),
        ),
        out_specs=(P("dp", "space", None, None), P("dp", "space", None, None)),
        check_vma=False,
    )
```
